128 devices in a mesh: tile: 16 (over z_lo, y, core), lev: 8 (over x, z_hi).
Axes of the slice: x: 4, y: 4, z: 4 (z_hi: 2, z_lo: 2; z = z_hi * 2 + z_lo), core: 2. Of those that a mesh axis runs over, the one named last changes fastest.
Arguments:
- adjoint_state: float32 [4, 88, 1024, 256], P(None, 'lev', 'tile'), may hold values from -6 to 6
- lower_coef: float32 [88, 1024, 256], P('lev', 'tile'), may hold values from 0.1 to 10
- upper_coef: float32 [88, 1024, 256], P('lev', 'tile'), may hold values from 0.1 to 10
- stencil_coef: float32 [4, 1024, 256], P(None, 'tile'), may hold values from 0.02 to 0.24
- land_mask: int32 [1024, 256], P('tile'), may hold values 0 or 1
Outputs:
- adjoint_input: float32 [4, 88, 1024, 256], P(None, 'lev', 'tile')
The draws below stay inside these ranges and needn't reach their ends.
All inputs are finite; a program needn't handle non-finite values. No bound on the sum of `land_mask` on one device may be relied on, other than what follows from the above.
Results may differ from the reference program's by a relative error of at most 0.00002.
Values sent between devices are 32-bit elements; how exact they have to be, the bound alone decides.
A program may use at most 256 MiB of HBM per device.

```python
import math
import jax
import jax.numpy as jnp
from jax import lax

NLEV = 88
TY = 256
FIELDS = 4
NX = 1024


def set_ends(drawn, own_key, least, top_value):
    spot = [jax.random.randint(jax.random.fold_in(own_key, axis), (), 0, length) for axis, length in enumerate(drawn.shape)]
    longest = drawn.shape.index(max(drawn.shape))
    neighbour = spot[:longest] + [(spot[longest] + 1) % drawn.shape[longest]] + spot[longest + 1:]
    return drawn.at[tuple(spot)].set(least).at[tuple(neighbour)].set(top_value)


def block_levels(own_key, extent, pieces, least, top_value):
    def one(axis_at, parts):
        steps = jax.random.uniform(jax.random.fold_in(jax.random.fold_in(own_key, 6), axis_at), (parts,), jnp.float32, least / len(pieces), top_value / len(pieces))
        return jnp.repeat(jnp.exp(steps), extent[axis_at] // parts).reshape((-1,) + (1,) * (len(extent) - axis_at - 1))

    loudness = one(*pieces[0])
    for cut in pieces[1:]:
        loudness = loudness * one(*cut)
    return loudness


def centred(key, shape, scale, most, shards=(), kind=jnp.bfloat16):
    array = scale * jax.random.normal(key, shape, jnp.float32)
    if shards:
        array = array * block_levels(key, shape, shards, -0.22, 0.18)
    return jnp.clip(array, -most, most).astype(kind)


def setup_inputs(seed: int = 0) -> dict:
    arg_keys = jax.random.split(jax.random.key(seed), 6)
    return {
        "adjoint_state": centred(arg_keys[0], (FIELDS, NLEV, NX, TY), 1.0, 6.0, ((1, 8), (2, 16)), jnp.float32),
        "lower_coef": jnp.clip(jnp.exp(math.log(10.0) - 4.6051702 * jax.random.uniform(arg_keys[1], (NLEV, NX, TY), jnp.float32) ** block_levels(arg_keys[1], (NLEV, NX, TY), ((0, 8), (1, 16)), -0.2, 0.2)), 0.1, 10.0),
        "upper_coef": jnp.clip(jnp.exp(math.log(10.0) - 4.6051702 * jax.random.uniform(arg_keys[2], (NLEV, NX, TY), jnp.float32) ** block_levels(arg_keys[2], (NLEV, NX, TY), ((0, 8), (1, 16)), -0.2, 0.2)), 0.1, 10.0),
        "stencil_coef": jnp.clip(jnp.exp(math.log(0.24) - 2.4849066 * jax.random.uniform(arg_keys[3], (4, NX, TY), jnp.float32) ** block_levels(arg_keys[3], (4, NX, TY), ((1, 16),), -0.2, 0.2)), 0.02, 0.24),
        "land_mask": set_ends((jax.random.randint(arg_keys[4], (NX, TY), 0, 5) < 4).astype(jnp.int32), jax.random.fold_in(arg_keys[4], 1), 0, 1),
    }


def thomas(lower, upper, rhs):
    zero_row = jnp.zeros_like(lower[:1])
    low = jnp.concatenate([zero_row, lower[1:]], 0)
    upp = jnp.concatenate([upper[:-1], zero_row], 0)
    diag = 1.0 + low + upp
    sub = jnp.concatenate([zero_row, -upp[:-1]], 0)
    sup = jnp.concatenate([-low[1:], zero_row], 0)
    right = jnp.moveaxis(rhs, 1, 0)

    def forward(carry, item):
        prev_c, prev_r = carry
        s_k, d_k, u_k, r_k = item
        denom = d_k - s_k * prev_c
        next_c = u_k / denom
        next_r = (r_k - s_k[None] * prev_r) / denom[None]
        return (next_c, next_r), (next_c, next_r)

    init = (jnp.zeros_like(diag[0]), jnp.zeros_like(right[0]))
    unused, (coefs, rights) = lax.scan(forward, init, (sub, diag, sup, right))

    def backward(carry, item):
        c_k, r_k = item
        value = r_k - c_k[None] * carry
        return value, value

    unused2, values = lax.scan(backward, jnp.zeros_like(right[0]), (coefs, rights), reverse=True)
    return jnp.moveaxis(values, 0, 1)


def horizontal(solved, stencil_coef):
    east, west, north, south = stencil_coef[0], stencil_coef[1], stencil_coef[2], stencil_coef[3]
    total = east + west + north + south
    result = solved * (1.0 - total)
    east_term = jnp.pad((solved * east)[:, :, :-1], ((0, 0), (0, 0), (1, 0), (0, 0)))
    west_term = jnp.pad((solved * west)[:, :, 1:], ((0, 0), (0, 0), (0, 1), (0, 0)))
    north_term = jnp.pad((solved * north)[:, :, :, :-1], ((0, 0), (0, 0), (0, 0), (1, 0)))
    south_term = jnp.pad((solved * south)[:, :, :, 1:], ((0, 0), (0, 0), (0, 0), (0, 1)))
    return result + east_term + west_term + north_term + south_term


def reference(adjoint_state, lower_coef, upper_coef, stencil_coef, land_mask):
    fields, levels, rows, cols = adjoint_state.shape
    masked = adjoint_state * land_mask.astype(adjoint_state.dtype)[None, None]
    solved = thomas(lower_coef.reshape(levels, rows * cols), upper_coef.reshape(levels, rows * cols),
                    masked.reshape(fields, levels, rows * cols))
    return horizontal(solved.reshape(fields, levels, rows, cols), stencil_coef)
```

```python
import functools

import jax
import jax.numpy as jnp
from jax import lax
from jax.experimental import pallas as pl
from jax.experimental.pallas import tpu as pltpu
from jax.sharding import PartitionSpec as P

MESH = pl.DeviceIdType.MESH
N = 8
FIELDS = 4
LEVELS = 11
ROWS, COLS = 64, 256
LANES = 128
PAD = 8
HEIGHT = ROWS + 2 * PAD
STACK = FIELDS * LEVELS
QUARTER = 16
PLANES = 4 + 2 * FIELDS
BACK = 2 * FIELDS


def quarter_row(i):
    return pl.multiple_of(QUARTER * lax.rem(3 * i, 4), QUARTER)


def kernel(
    adj, low, upp, sten, mask, out,
    m_v, a_v, b_v, s_v, k_v, co_v, x_v, snd, rcv, rts, rtr, hs, hr,
    load_sem, small_sem, fs, fr, fl, bs, br, bl, hss, hrs,
):
    tile = lax.axis_index("tile")
    lev = lax.axis_index("lev")
    tiles = lax.axis_size("tile")

    def loads(i):
        rows = pl.ds(quarter_row(i), QUARTER)
        return (
            pltpu.make_async_copy(adj.at[:, :, rows, :], m_v.at[:, :, rows, :], load_sem.at[i, 0]),
            pltpu.make_async_copy(low.at[:, rows, :], a_v.at[:, rows, :], load_sem.at[i, 1]),
            pltpu.make_async_copy(upp.at[:, rows, :], b_v.at[:, rows, :], load_sem.at[i, 2]),
        )

    load_mask = pltpu.make_async_copy(mask, k_v, small_sem.at[0])
    load_sten = pltpu.make_async_copy(sten, s_v, small_sem.at[1])
    load_mask.start()
    for i in range(4):
        for c in loads(i):
            c.start()
    load_sten.start()

    barrier = pltpu.get_barrier_semaphore()
    for off in range(1, N):
        pl.semaphore_signal(barrier, inc=1, device_id=(tile, lax.rem(lev + off, N)), device_id_type=MESH)
    right, left = lax.rem(tile + 1, tiles), lax.rem(tile + tiles - 1, tiles)
    for t in (right, left):
        pl.semaphore_signal(barrier, inc=1, device_id=(t, lev), device_id_type=MESH)

    first = jnp.where(lev == 0, 0.0, 1.0)
    last = jnp.where(lev == N - 1, 0.0, 1.0)

    def eliminate(i, carry):
        for c in loads(i):
            c.wait()
        start = quarter_row(i)
        rows = pl.ds(start, QUARTER)
        half, base = lax.div(i, 2), lax.rem(i, 2) * 4
        keep = k_v[rows, :].astype(jnp.float32)
        r = [None] * FIELDS
        p = [None] * FIELDS
        a = a_v[0, rows, :] * first
        chain = a
        inv = g = q = b = None
        for k in range(LEVELS):
            b_next = b_v[k, rows, :]
            if k == LEVELS - 1:
                b_next = b_next * last
            d = 1.0 + a + b_next
            if k:
                d = d - b * a * inv
            inv = 1.0 / d
            if k:
                h = b * inv
                g = h * g
                q = q + chain * g
            else:
                g = inv
                q = chain * g
            for f in range(FIELDS):
                m = m_v[f, k, rows, :] * keep
                if k:
                    r[f] = m * inv + h * r[f]
                    p[f] = p[f] + chain * r[f]
                else:
                    r[f] = m * inv
                    p[f] = chain * r[f]
                m_v[f, k, rows, :] = r[f]
            if k < LEVELS - 1:
                a = a_v[k + 1, rows, :]
                e = a * inv
            else:
                e = inv
            chain = chain * e
            a_v[k, rows, :] = e
            b_v[k, rows, :] = g
            b = b_next
        planes = [b * inv] + [b * r[f] for f in range(FIELDS)] + [chain, b * g, q] + p
        for j in range(4):
            row, col = (j // 2) * 8, (j % 2) * LANES
            for n, plane in enumerate(planes):
                snd[half, base + j, n] = plane[row:row + 8, col:col + LANES]
        return carry

    def forward(half, to):
        return pltpu.make_async_remote_copy(
            src_ref=snd.at[half, to], dst_ref=rcv.at[half, lev], send_sem=fs.at[half, to], recv_sem=fr.at[half, lev],
            device_id=(tile, to), device_id_type=MESH)

    def forward_from(half, source):
        return pltpu.make_async_remote_copy(
            src_ref=snd.at[half, source], dst_ref=rcv.at[half, source], send_sem=fs.at[half, source],
            recv_sem=fr.at[half, source], device_id=(tile, source), device_id_type=MESH)

    def backward(half, to):
        return pltpu.make_async_remote_copy(
            src_ref=rts.at[half, to], dst_ref=rtr.at[half, lev], send_sem=bs.at[half, to], recv_sem=br.at[half, lev],
            device_id=(tile, to), device_id_type=MESH)

    def backward_from(half, source):
        return pltpu.make_async_remote_copy(
            src_ref=rts.at[half, source], dst_ref=rtr.at[half, source], send_sem=bs.at[half, source],
            recv_sem=br.at[half, source], device_id=(tile, source), device_id_type=MESH)

    def own_forward(half):
        return pltpu.make_async_copy(snd.at[half, lev], rcv.at[half, lev], fl.at[half])

    def own_backward(half):
        return pltpu.make_async_copy(rts.at[half, lev], rtr.at[half, lev], bl.at[half])

    def send_forward(half):
        own_forward(half).start()
        for off in range(1, N):
            forward(half, lax.rem(lev + off, N)).start()

    load_mask.wait()
    lax.fori_loop(0, 2, eliminate, 0)
    load_sten.wait()
    pl.semaphore_wait(barrier, N + 1)
    send_forward(0)
    lax.fori_loop(2, 4, eliminate, 0)
    send_forward(1)

    row = lax.broadcasted_iota(jnp.int32, (ROWS, LANES), 0)
    lane = lax.broadcasted_iota(jnp.int32, (ROWS, LANES), 1)
    has_left = jnp.where(tile == 0, 0.0, 1.0)
    has_right = jnp.where(tile == tiles - 1, 0.0, 1.0)
    for c in range(2):
        cols = pl.ds(c * LANES, LANES)
        east, west, north, south = s_v[0, :, cols], s_v[1, :, cols], s_v[2, :, cols], s_v[3, :, cols]
        co_v[0, c] = 1.0 - (east + west + north + south)
        co_v[1, c] = jnp.where(row == 0, has_left, pltpu.roll(east, 1, 0))
        co_v[2, c] = jnp.where(row == ROWS - 1, has_right, pltpu.roll(west, ROWS - 1, 0))
        before = 0.0 if c == 0 else pltpu.roll(s_v[2, :, :LANES], 1, 1)
        after = pltpu.roll(s_v[3, :, LANES:], LANES - 1, 1) if c == 0 else 0.0
        co_v[3, c] = jnp.where(lane == 0, before, pltpu.roll(north, 1, 1))
        co_v[4, c] = jnp.where(lane == LANES - 1, after, pltpu.roll(south, LANES - 1, 1))

    def solve(half, carry):
        own_forward(half).wait()
        for off in range(1, N):
            forward_from(half, lax.rem(lev + off, N)).wait_recv()
        fields = range(FIELDS)
        flux = [rcv[half, 0, 1 + f] for f in fields]
        slope = rcv[half, 0, 0]
        into, gain = [None] * N, [None] * N
        for s in range(1, N):
            dd, bb, cc, aa = rcv[half, s, 0], rcv[half, s, 5], rcv[half, s, 6], rcv[half, s, 7]
            inv = 1.0 / (1.0 - slope * aa)
            into[s] = [(flux[f] + slope * rcv[half, s, 8 + f]) * inv for f in fields]
            if s < N - 1:
                gain[s] = slope * bb * inv
                flux = [rcv[half, s, 1 + f] + cc * into[s][f] for f in fields]
                slope = dd + cc * gain[s]
        zero = jnp.zeros((8, LANES), jnp.float32)
        v = [zero] * FIELDS
        for s in range(N - 1, -1, -1):
            if s == 0:
                u = [zero] * FIELDS
            elif s == N - 1:
                u = into[s]
            else:
                u = [into[s][f] + gain[s] * v[f] for f in fields]
            for f in fields:
                rts[half, s, f] = u[f]
                rts[half, s, FIELDS + f] = v[f]
            if s:
                aa, bb = rcv[half, s, 7], rcv[half, s, 5]
                v = [rcv[half, s, 8 + f] + aa * u[f] + bb * v[f] for f in fields]
        own_backward(half).start()
        for off in range(1, N):
            backward(half, lax.rem(lev + off, N)).start()
        return carry

    lax.fori_loop(0, 2, solve, 0)

    def spot(fk, c, r):
        return (fk * 2 + c) * HEIGHT + PAD + r

    def substitute(half):
        own_backward(half).wait()
        for off in range(1, N):
            backward_from(half, lax.rem(lev + off, N)).wait_recv()

        def block(j, carry):
            start = pl.multiple_of(quarter_row(half * 2 + lax.div(j, 2)) + 8 * lax.rem(j, 2), 8)
            rows = pl.ds(start, 8)
            for c in range(2):
                cols = pl.ds(c * LANES, LANES)
                x = [None] * FIELDS
                for k in range(LEVELS - 1, -1, -1):
                    e, g = a_v[k, rows, cols], b_v[k, rows, cols]
                    for f in range(FIELDS):
                        u = rtr[half, 2 * j + c, f]
                        beyond = rtr[half, 2 * j + c, FIELDS + f] if k == LEVELS - 1 else x[f]
                        x[f] = m_v[f, k, rows, cols] + g * u + e * beyond
                        at = pl.multiple_of(spot(f * LEVELS + k, c, start), 8)
                        x_v[pl.ds(at, 8), :] = x[f]
            return carry

        lax.fori_loop(0, 4, block, 0)

    def halo(way):
        to = right if way == 0 else left
        return pltpu.make_async_remote_copy(
            src_ref=hs.at[way], dst_ref=hr.at[way], send_sem=hss.at[way], recv_sem=hrs.at[way],
            device_id=(to, lev), device_id_type=MESH)

    def every(c, r):
        return pl.ds(spot(0, c, r), STACK, stride=2 * HEIGHT)

    substitute(0)
    for way, r in ((0, ROWS - 1), (1, 0)):
        for c in range(2):
            weight = s_v[way, r:r + 1, c * LANES:(c + 1) * LANES]
            hs[way, c] = x_v[every(c, r), :] * weight
        halo(way).start()
    substitute(1)
    for way, r in ((0, -1), (1, ROWS)):
        halo(way).wait()
        for c in range(2):
            x_v[every(c, r), :] = hr[way, c]

    lane8 = lax.broadcasted_iota(jnp.int32, (8, LANES), 1)

    def transport(j, carry):
        start = pl.multiple_of(j * 8, 8)
        rows = pl.ds(start, 8)
        co = [[co_v[n, c, rows, :] for c in range(2)] for n in range(5)]

        def one(fk, inner):
            f, k = lax.div(fk, LEVELS), lax.rem(fk, LEVELS)
            at = [pl.multiple_of(spot(fk, c, start), 8) for c in range(2)]
            x = [x_v[pl.ds(at[c], 8), :] for c in range(2)]
            up = [x_v[pl.ds(at[c] - 1, 8), :] for c in range(2)]
            down = [x_v[pl.ds(at[c] + 1, 8), :] for c in range(2)]
            fwd = [pltpu.roll(x[c], 1, 1) for c in range(2)]
            bwd = [pltpu.roll(x[c], LANES - 1, 1) for c in range(2)]
            fwd[1] = jnp.where(lane8 == 0, fwd[0], fwd[1])
            bwd[0] = jnp.where(lane8 == LANES - 1, bwd[1], bwd[0])
            for c in range(2):
                total = x[c] * co[0][c] + up[c] * co[1][c] + down[c] * co[2][c]
                total = total + fwd[c] * co[3][c] + bwd[c] * co[4][c]
                out[f, k, rows, pl.ds(c * LANES, LANES)] = total
            return inner

        return lax.fori_loop(0, STACK, one, carry, unroll=4)

    lax.fori_loop(0, ROWS // 8, transport, 0)

    for half in range(2):
        for off in range(1, N):
            to = lax.rem(lev + off, N)
            forward(half, to).wait_send()
            backward(half, to).wait_send()


def per_device(adjoint_state, lower_coef, upper_coef, stencil_coef, land_mask):
    f32 = jnp.float32
    dma = pltpu.SemaphoreType.DMA
    return pl.pallas_call(
        kernel,
        out_shape=jax.ShapeDtypeStruct(adjoint_state.shape, f32),
        in_specs=[pl.BlockSpec(memory_space=pl.ANY)] * 5,
        out_specs=pl.BlockSpec(memory_space=pltpu.VMEM),
        scratch_shapes=[
            pltpu.VMEM((FIELDS, LEVELS, ROWS, COLS), f32),
            pltpu.VMEM((LEVELS, ROWS, COLS), f32),
            pltpu.VMEM((LEVELS, ROWS, COLS), f32),
            pltpu.VMEM((4, ROWS, COLS), f32),
            pltpu.VMEM((ROWS, COLS), jnp.int32),
            pltpu.VMEM((5, 2, ROWS, LANES), f32),
            pltpu.VMEM((STACK * 2 * HEIGHT, LANES), f32),
            pltpu.VMEM((2, N, PLANES, 8, LANES), f32),
            pltpu.VMEM((2, N, PLANES, 8, LANES), f32),
            pltpu.VMEM((2, N, BACK, 8, LANES), f32),
            pltpu.VMEM((2, N, BACK, 8, LANES), f32),
            pltpu.VMEM((2, 2, STACK, LANES), f32),
            pltpu.VMEM((2, 2, STACK, LANES), f32),
            dma((4, 3)),
            dma((2,)),
            dma((2, N)),
            dma((2, N)),
            dma((2,)),
            dma((2, N)),
            dma((2, N)),
            dma((2,)),
            dma((2,)),
            dma((2,)),
        ],
        compiler_params=pltpu.CompilerParams(
            collective_id=0, has_side_effects=True, vmem_limit_bytes=40 * 2**20),
    )(adjoint_state, lower_coef, upper_coef, stencil_coef, land_mask)


def solution(mesh):
    return jax.shard_map(
        per_device,
        mesh=mesh,
        in_specs=(
            P(None, "lev", "tile", None),
            P("lev", "tile", None),
            P("lev", "tile", None),
            P(None, "tile", None),
            P("tile", None),
        ),
        out_specs=P(None, "lev", "tile", None),
        check_vma=False,
    )
```

```python
import functools

import jax
import jax.numpy as jnp
from jax import lax
from jax.experimental import pallas as pl
from jax.experimental.pallas import tpu as pltpu
from jax.sharding import PartitionSpec as P

MESH = pl.DeviceIdType.MESH
N = 8
FIELDS = 4
LEVELS = 11
ROWS, COLS = 64, 256
LANES = 128
PAD = 8
HEIGHT = ROWS + 2 * PAD
STACK = FIELDS * LEVELS
QUARTER = 16
PLANES = 4 + 2 * FIELDS
BACK = 2 * FIELDS


def quarter_row(i):
    return pl.multiple_of(QUARTER * lax.rem(3 * i, 4), QUARTER)


def kernel(
    adj, low, upp, sten, mask, out,
    m_v, a_v, b_v, s_v, k_v, co_v, x_v, snd, rcv, rts, rtr, hs, hr,
    load_sem, small_sem, fs, fr, fl, bs, br, bl, hss, hrs,
):
    tile = lax.axis_index("tile")
    lev = lax.axis_index("lev")
    tiles = lax.axis_size("tile")

    def loads(i):
        rows = pl.ds(quarter_row(i), QUARTER)
        return (
            pltpu.make_async_copy(adj.at[:, :, rows, :], m_v.at[:, :, rows, :], load_sem.at[i, 0]),
            pltpu.make_async_copy(low.at[:, rows, :], a_v.at[:, rows, :], load_sem.at[i, 1]),
            pltpu.make_async_copy(upp.at[:, rows, :], b_v.at[:, rows, :], load_sem.at[i, 2]),
        )

    load_mask = pltpu.make_async_copy(mask, k_v, small_sem.at[0])
    load_sten = pltpu.make_async_copy(sten, s_v, small_sem.at[1])
    load_mask.start()
    for i in range(4):
        for c in loads(i):
            c.start()
    load_sten.start()

    barrier = pltpu.get_barrier_semaphore()
    for off in range(1, N):
        pl.semaphore_signal(barrier, inc=1, device_id=(tile, lax.rem(lev + off, N)), device_id_type=MESH)
    right, left = lax.rem(tile + 1, tiles), lax.rem(tile + tiles - 1, tiles)
    for t in (right, left):
        pl.semaphore_signal(barrier, inc=1, device_id=(t, lev), device_id_type=MESH)

    first = jnp.where(lev == 0, 0.0, 1.0)
    last = jnp.where(lev == N - 1, 0.0, 1.0)

    def eliminate(i, carry):
        for c in loads(i):
            c.wait()
        start = quarter_row(i)
        rows = pl.ds(start, QUARTER)
        half, base = lax.div(i, 2), lax.rem(i, 2) * 4
        keep = k_v[rows, :].astype(jnp.float32)
        r = [None] * FIELDS
        p = [None] * FIELDS
        a = a_v[0, rows, :] * first
        chain = a
        inv = g = q = b = None
        for k in range(LEVELS):
            b_next = b_v[k, rows, :]
            if k == LEVELS - 1:
                b_next = b_next * last
            d = 1.0 + a + b_next
            if k:
                d = d - b * a * inv
            inv = 1.0 / d
            if k:
                h = b * inv
                g = h * g
                q = q + chain * g
            else:
                g = inv
                q = chain * g
            for f in range(FIELDS):
                m = m_v[f, k, rows, :] * keep
                if k:
                    r[f] = m * inv + h * r[f]
                    p[f] = p[f] + chain * r[f]
                else:
                    r[f] = m * inv
                    p[f] = chain * r[f]
                m_v[f, k, rows, :] = r[f]
            if k < LEVELS - 1:
                a = a_v[k + 1, rows, :]
                e = a * inv
            else:
                e = inv
            chain = chain * e
            a_v[k, rows, :] = e
            b_v[k, rows, :] = g
            b = b_next
        planes = [b * inv] + [b * r[f] for f in range(FIELDS)] + [chain, b * g, q] + p
        for j in range(4):
            row, col = (j // 2) * 8, (j % 2) * LANES
            for n, plane in enumerate(planes):
                snd[half, base + j, n] = plane[row:row + 8, col:col + LANES]
        return carry

    def forward(half, to):
        return pltpu.make_async_remote_copy(
            src_ref=snd.at[half, to], dst_ref=rcv.at[half, lev], send_sem=fs.at[half, to], recv_sem=fr.at[half, lev],
            device_id=(tile, to), device_id_type=MESH)

    def forward_from(half, source):
        return pltpu.make_async_remote_copy(
            src_ref=snd.at[half, source], dst_ref=rcv.at[half, source], send_sem=fs.at[half, source],
            recv_sem=fr.at[half, source], device_id=(tile, source), device_id_type=MESH)

    def backward(half, to):
        return pltpu.make_async_remote_copy(
            src_ref=rts.at[half, to], dst_ref=rtr.at[half, lev], send_sem=bs.at[half, to], recv_sem=br.at[half, lev],
            device_id=(tile, to), device_id_type=MESH)

    def backward_from(half, source):
        return pltpu.make_async_remote_copy(
            src_ref=rts.at[half, source], dst_ref=rtr.at[half, source], send_sem=bs.at[half, source],
            recv_sem=br.at[half, source], device_id=(tile, source), device_id_type=MESH)

    def own_forward(half):
        return pltpu.make_async_copy(snd.at[half, lev], rcv.at[half, lev], fl.at[half])

    def own_backward(half):
        return pltpu.make_async_copy(rts.at[half, lev], rtr.at[half, lev], bl.at[half])

    def send_forward(half):
        own_forward(half).start()
        for off in range(1, N):
            forward(half, lax.rem(lev + off, N)).start()

    load_mask.wait()
    lax.fori_loop(0, 2, eliminate, 0)
    load_sten.wait()
    pl.semaphore_wait(barrier, N + 1)
    send_forward(0)
    lax.fori_loop(2, 4, eliminate, 0)
    send_forward(1)

    row = lax.broadcasted_iota(jnp.int32, (ROWS, LANES), 0)
    lane = lax.broadcasted_iota(jnp.int32, (ROWS, LANES), 1)
    has_left = jnp.where(tile == 0, 0.0, 1.0)
    has_right = jnp.where(tile == tiles - 1, 0.0, 1.0)
    for c in range(2):
        cols = pl.ds(c * LANES, LANES)
        east, west, north, south = s_v[0, :, cols], s_v[1, :, cols], s_v[2, :, cols], s_v[3, :, cols]
        co_v[0, c] = 1.0 - (east + west + north + south)
        co_v[1, c] = jnp.where(row == 0, has_left, pltpu.roll(east, 1, 0))
        co_v[2, c] = jnp.where(row == ROWS - 1, has_right, pltpu.roll(west, ROWS - 1, 0))
        before = 0.0 if c == 0 else pltpu.roll(s_v[2, :, :LANES], 1, 1)
        after = pltpu.roll(s_v[3, :, LANES:], LANES - 1, 1) if c == 0 else 0.0
        co_v[3, c] = jnp.where(lane == 0, before, pltpu.roll(north, 1, 1))
        co_v[4, c] = jnp.where(lane == LANES - 1, after, pltpu.roll(south, LANES - 1, 1))

    def solve(half, carry):
        own_forward(half).wait()
        for off in range(1, N):
            forward_from(half, lax.rem(lev + off, N)).wait_recv()
        fields = range(FIELDS)
        flux = [rcv[half, 0, 1 + f] for f in fields]
        slope = rcv[half, 0, 0]
        into, gain = [None] * N, [None] * N
        for s in range(1, N):
            dd, bb, cc, aa = rcv[half, s, 0], rcv[half, s, 5], rcv[half, s, 6], rcv[half, s, 7]
            inv = 1.0 / (1.0 - slope * aa)
            into[s] = [(flux[f] + slope * rcv[half, s, 8 + f]) * inv for f in fields]
            if s < N - 1:
                gain[s] = slope * bb * inv
                flux = [rcv[half, s, 1 + f] + cc * into[s][f] for f in fields]
                slope = dd + cc * gain[s]
        zero = jnp.zeros((8, LANES), jnp.float32)
        v = [zero] * FIELDS
        for s in range(N - 1, -1, -1):
            if s == 0:
                u = [zero] * FIELDS
            elif s == N - 1:
                u = into[s]
            else:
                u = [into[s][f] + gain[s] * v[f] for f in fields]
            for f in fields:
                rts[half, s, f] = u[f]
                rts[half, s, FIELDS + f] = v[f]
            if s:
                aa, bb = rcv[half, s, 7], rcv[half, s, 5]
                v = [rcv[half, s, 8 + f] + aa * u[f] + bb * v[f] for f in fields]
        own_backward(half).start()
        for off in range(1, N):
            backward(half, lax.rem(lev + off, N)).start()
        return carry

    lax.fori_loop(0, 2, solve, 0)

    def spot(fk, c, r):
        return (fk * 2 + c) * HEIGHT + PAD + r

    def substitute(half):
        own_backward(half).wait()
        for off in range(1, N):
            backward_from(half, lax.rem(lev + off, N)).wait_recv()

        def block(j, carry):
            start = pl.multiple_of(quarter_row(half * 2 + lax.div(j, 2)) + 8 * lax.rem(j, 2), 8)
            rows = pl.ds(start, 8)
            for c in range(2):
                cols = pl.ds(c * LANES, LANES)
                x = [None] * FIELDS
                for k in range(LEVELS - 1, -1, -1):
                    e, g = a_v[k, rows, cols], b_v[k, rows, cols]
                    for f in range(FIELDS):
                        u = rtr[half, 2 * j + c, f]
                        beyond = rtr[half, 2 * j + c, FIELDS + f] if k == LEVELS - 1 else x[f]
                        x[f] = m_v[f, k, rows, cols] + g * u + e * beyond
                        at = pl.multiple_of(spot(f * LEVELS + k, c, start), 8)
                        x_v[pl.ds(at, 8), :] = x[f]
            return carry

        lax.fori_loop(0, 4, block, 0)

    def halo(way):
        to = right if way == 0 else left
        return pltpu.make_async_remote_copy(
            src_ref=hs.at[way], dst_ref=hr.at[way], send_sem=hss.at[way], recv_sem=hrs.at[way],
            device_id=(to, lev), device_id_type=MESH)

    def every(c, r):
        return pl.ds(spot(0, c, r), STACK, stride=2 * HEIGHT)

    substitute(0)
    for way, r in ((0, ROWS - 1), (1, 0)):
        for c in range(2):
            weight = s_v[way, r:r + 1, c * LANES:(c + 1) * LANES]
            hs[way, c] = x_v[every(c, r), :] * weight
        halo(way).start()
    substitute(1)
    for way, r in ((0, -1), (1, ROWS)):
        halo(way).wait()
        for c in range(2):
            x_v[every(c, r), :] = hr[way, c]

    lane8 = lax.broadcasted_iota(jnp.int32, (8, LANES), 1)

    def transport(j, carry):
        start = pl.multiple_of(j * 8, 8)
        rows = pl.ds(start, 8)
        co = [[co_v[n, c, rows, :] for c in range(2)] for n in range(5)]

        def one(fk, inner):
            f, k = lax.div(fk, LEVELS), lax.rem(fk, LEVELS)
            at = [pl.multiple_of(spot(fk, c, start), 8) for c in range(2)]
            x = [x_v[pl.ds(at[c], 8), :] for c in range(2)]
            up = [x_v[pl.ds(at[c] - 1, 8), :] for c in range(2)]
            down = [x_v[pl.ds(at[c] + 1, 8), :] for c in range(2)]
            fwd = [pltpu.roll(x[c], 1, 1) for c in range(2)]
            bwd = [pltpu.roll(x[c], LANES - 1, 1) for c in range(2)]
            fwd[1] = jnp.where(lane8 == 0, fwd[0], fwd[1])
            bwd[0] = jnp.where(lane8 == LANES - 1, bwd[1], bwd[0])
            for c in range(2):
                total = x[c] * co[0][c] + up[c] * co[1][c] + down[c] * co[2][c]
                total = total + fwd[c] * co[3][c] + bwd[c] * co[4][c]
                out[f, k, rows, pl.ds(c * LANES, LANES)] = total
            return inner

        return lax.fori_loop(0, STACK, one, carry, unroll=22)

    lax.fori_loop(0, ROWS // 8, transport, 0)

    for half in range(2):
        for off in range(1, N):
            to = lax.rem(lev + off, N)
            forward(half, to).wait_send()
            backward(half, to).wait_send()


def per_device(adjoint_state, lower_coef, upper_coef, stencil_coef, land_mask):
    f32 = jnp.float32
    dma = pltpu.SemaphoreType.DMA
    return pl.pallas_call(
        kernel,
        out_shape=pltpu.VMEM(adjoint_state.shape, f32),
        in_specs=[pl.BlockSpec(memory_space=pltpu.HBM)] * 5,
        out_specs=pl.BlockSpec(memory_space=pltpu.VMEM),
        scratch_shapes=[
            pltpu.VMEM((FIELDS, LEVELS, ROWS, COLS), f32),
            pltpu.VMEM((LEVELS, ROWS, COLS), f32),
            pltpu.VMEM((LEVELS, ROWS, COLS), f32),
            pltpu.VMEM((4, ROWS, COLS), f32),
            pltpu.VMEM((ROWS, COLS), jnp.int32),
            pltpu.VMEM((5, 2, ROWS, LANES), f32),
            pltpu.VMEM((STACK * 2 * HEIGHT, LANES), f32),
            pltpu.VMEM((2, N, PLANES, 8, LANES), f32),
            pltpu.VMEM((2, N, PLANES, 8, LANES), f32),
            pltpu.VMEM((2, N, BACK, 8, LANES), f32),
            pltpu.VMEM((2, N, BACK, 8, LANES), f32),
            pltpu.VMEM((2, 2, STACK, LANES), f32),
            pltpu.VMEM((2, 2, STACK, LANES), f32),
            dma((4, 3)),
            dma((2,)),
            dma((2, N)),
            dma((2, N)),
            dma((2,)),
            dma((2, N)),
            dma((2, N)),
            dma((2,)),
            dma((2,)),
            dma((2,)),
        ],
        compiler_params=pltpu.CompilerParams(
            collective_id=0, has_side_effects=True, vmem_limit_bytes=40 * 2**20),
    )(*(pltpu.with_memory_space_constraint(x, pltpu.HBM) for x in (
        adjoint_state, lower_coef, upper_coef, stencil_coef, land_mask)))


def solution(mesh):
    return jax.shard_map(
        per_device,
        mesh=mesh,
        in_specs=(
            P(None, "lev", "tile", None),
            P("lev", "tile", None),
            P("lev", "tile", None),
            P(None, "tile", None),
            P("tile", None),
        ),
        out_specs=P(None, "lev", "tile", None),
        check_vma=False,
    )
```

```python
import functools

import jax
import jax.numpy as jnp
from jax import lax
from jax.experimental import pallas as pl
from jax.experimental.pallas import tpu as pltpu
from jax.sharding import PartitionSpec as P

MESH = pl.DeviceIdType.MESH
N = 8
FIELDS = 4
LEVELS = 11
ROWS, COLS = 64, 256
LANES = 128
PAD = 8
HEIGHT = ROWS + 2 * PAD
STACK = FIELDS * LEVELS
QUARTER = 16
PLANES = 4 + 2 * FIELDS
BACK = 2 * FIELDS
FORWARD = (slice(0, 1 + FIELDS), slice(0, PLANES), slice(PLANES - 1 - FIELDS, PLANES))
BACKWARD = (slice(FIELDS, BACK), slice(0, BACK), slice(0, FIELDS))


def quarter_row(i):
    return pl.multiple_of(QUARTER * lax.rem(3 * i, 4), QUARTER)


def solver(group, j):
    return 2 * j + lax.rem(group + j, 2)


def kernel(
    adj, low, upp, sten, mask, out,
    m_v, a_v, b_v, s_v, k_v, co_v, x_v, snd, rcv, rts, rtr, hs, hr,
    load_sem, small_sem, fs, fr, fl, bs, br, bl, hss, hrs,
):
    tile = lax.axis_index("tile")
    lev = lax.axis_index("lev")
    tiles = lax.axis_size("tile")

    def loads(i):
        rows = pl.ds(quarter_row(i), QUARTER)
        return (
            pltpu.make_async_copy(adj.at[:, :, rows, :], m_v.at[:, :, rows, :], load_sem.at[i, 0]),
            pltpu.make_async_copy(low.at[:, rows, :], a_v.at[:, rows, :], load_sem.at[i, 1]),
            pltpu.make_async_copy(upp.at[:, rows, :], b_v.at[:, rows, :], load_sem.at[i, 2]),
        )

    load_mask = pltpu.make_async_copy(mask, k_v, small_sem.at[0])
    load_sten = pltpu.make_async_copy(sten, s_v, small_sem.at[1])
    load_mask.start()
    for i in range(4):
        for c in loads(i):
            c.start()
    load_sten.start()

    barrier = pltpu.get_barrier_semaphore()
    for off in range(1, N):
        pl.semaphore_signal(barrier, inc=1, device_id=(tile, lax.rem(lev + off, N)), device_id_type=MESH)
    right, left = lax.rem(tile + 1, tiles), lax.rem(tile + tiles - 1, tiles)
    for t in (right, left):
        pl.semaphore_signal(barrier, inc=1, device_id=(t, lev), device_id_type=MESH)

    @pl.when(lev == 0)
    def _():
        rtr[:, :, :FIELDS] = jnp.zeros((2, N, FIELDS, 8, LANES), jnp.float32)

    @pl.when(lev == N - 1)
    def _():
        rtr[:, :, FIELDS:] = jnp.zeros((2, N, FIELDS, 8, LANES), jnp.float32)

    first = jnp.where(lev == 0, 0.0, 1.0)
    last = jnp.where(lev == N - 1, 0.0, 1.0)

    def eliminate(i):
        for c in loads(i):
            c.wait()
        start = quarter_row(i)
        rows = pl.ds(start, QUARTER)
        half, group = lax.div(i, 2), lax.rem(i, 2)
        keep = k_v[rows, :].astype(jnp.float32)
        r = [None] * FIELDS
        p = [None] * FIELDS
        a = a_v[0, rows, :] * first
        chain = a
        inv = g = q = b = None
        for k in range(LEVELS):
            b_next = b_v[k, rows, :]
            if k == LEVELS - 1:
                b_next = b_next * last
            d = 1.0 + a + b_next
            if k:
                d = d - b * a * inv
            inv = pltpu.reciprocal(d, approx=True)
            if k:
                h = b * inv
                g = h * g
                q = q + chain * g
            else:
                g = inv
                q = chain * g
            for f in range(FIELDS):
                m = m_v[f, k, rows, :] * keep
                if k:
                    r[f] = m * inv + h * r[f]
                    p[f] = p[f] + chain * r[f]
                else:
                    r[f] = m * inv
                    p[f] = chain * r[f]
                m_v[f, k, rows, :] = r[f]
            if k < LEVELS - 1:
                a = a_v[k + 1, rows, :]
                e = a * inv
            else:
                e = inv
            chain = chain * e
            a_v[k, rows, :] = e
            b_v[k, rows, :] = g
            b = b_next
        planes = [b * inv] + [b * r[f] for f in range(FIELDS)] + [chain, b * g, q] + p
        for j in range(4):
            row, col = (j // 2) * 8, (j % 2) * LANES
            for n, plane in enumerate(planes):
                snd[half, solver(group, j), n] = plane[row:row + 8, col:col + LANES]

    def forward(half, to, part):
        return pltpu.make_async_remote_copy(
            src_ref=snd.at[half, to, part], dst_ref=rcv.at[half, lev, part], send_sem=fs.at[half, to],
            recv_sem=fr.at[half, lev], device_id=(tile, to), device_id_type=MESH)

    def forward_from(half, source, part):
        return pltpu.make_async_remote_copy(
            src_ref=snd.at[half, source, part], dst_ref=rcv.at[half, source, part], send_sem=fs.at[half, source],
            recv_sem=fr.at[half, source], device_id=(tile, source), device_id_type=MESH)

    def backward(half, to, part):
        return pltpu.make_async_remote_copy(
            src_ref=rts.at[half, to, part], dst_ref=rtr.at[half, lev, part], send_sem=bs.at[half, to],
            recv_sem=br.at[half, lev], device_id=(tile, to), device_id_type=MESH)

    def backward_from(half, source, part):
        return pltpu.make_async_remote_copy(
            src_ref=rts.at[half, source, part], dst_ref=rtr.at[half, source, part], send_sem=bs.at[half, source],
            recv_sem=br.at[half, source], device_id=(tile, source), device_id_type=MESH)

    def own_forward(half):
        return pltpu.make_async_copy(snd.at[half, lev], rcv.at[half, lev], fl.at[half])

    def own_backward(half):
        return pltpu.make_async_copy(rts.at[half, lev], rtr.at[half, lev], bl.at[half])

    def by_slab(s, parts, run):
        pl.when(s == 0)(lambda: run(parts[0]))
        pl.when(s == N - 1)(lambda: run(parts[2]))
        pl.when((s != 0) & (s != N - 1))(lambda: run(parts[1]))

    def send_forward(i):
        half, group = lax.div(i, 2), lax.rem(i, 2)

        def run(part):
            for j in range(4):
                to = solver(group, j)
                pl.when(to != lev)(lambda: forward(half, to, part).start())

        by_slab(lev, FORWARD, run)
        for j in range(4):
            pl.when(solver(group, j) == lev)(lambda: own_forward(half).start())

    def quarter(i, carry):
        eliminate(i)
        pl.when(i == 0)(lambda: pl.semaphore_wait(barrier, N + 1))
        send_forward(i)
        return carry

    load_mask.wait()
    lax.fori_loop(0, 4, quarter, 0)
    load_sten.wait()

    row = lax.broadcasted_iota(jnp.int32, (ROWS, LANES), 0)
    lane = lax.broadcasted_iota(jnp.int32, (ROWS, LANES), 1)
    has_left = jnp.where(tile == 0, 0.0, 1.0)
    has_right = jnp.where(tile == tiles - 1, 0.0, 1.0)
    for c in range(2):
        cols = pl.ds(c * LANES, LANES)
        east, west, north, south = s_v[0, :, cols], s_v[1, :, cols], s_v[2, :, cols], s_v[3, :, cols]
        co_v[0, c] = 1.0 - (east + west + north + south)
        co_v[1, c] = jnp.where(row == 0, has_left, pltpu.roll(east, 1, 0))
        co_v[2, c] = jnp.where(row == ROWS - 1, has_right, pltpu.roll(west, ROWS - 1, 0))
        before = 0.0 if c == 0 else pltpu.roll(s_v[2, :, :LANES], 1, 1)
        after = pltpu.roll(s_v[3, :, LANES:], LANES - 1, 1) if c == 0 else 0.0
        co_v[3, c] = jnp.where(lane == 0, before, pltpu.roll(north, 1, 1))
        co_v[4, c] = jnp.where(lane == LANES - 1, after, pltpu.roll(south, LANES - 1, 1))

    def solve(half, carry):
        own_forward(half).wait()
        for s in range(N):
            part = FORWARD[0 if s == 0 else 2 if s == N - 1 else 1]
            pl.when(lev != s)(lambda: forward_from(half, s, part).wait_recv())
        fields = range(FIELDS)
        flux = [rcv[half, 0, 1 + f] for f in fields]
        slope = rcv[half, 0, 0]
        into, gain = [None] * N, [None] * N
        for s in range(1, N):
            aa = rcv[half, s, 7]
            inv = pltpu.reciprocal(1.0 - slope * aa, approx=True)
            into[s] = [(flux[f] + slope * rcv[half, s, 8 + f]) * inv for f in fields]
            if s < N - 1:
                dd, bb, cc = rcv[half, s, 0], rcv[half, s, 5], rcv[half, s, 6]
                gain[s] = slope * bb * inv
                flux = [rcv[half, s, 1 + f] + cc * into[s][f] for f in fields]
                slope = dd + cc * gain[s]
        zero = jnp.zeros((8, LANES), jnp.float32)
        v = [zero] * FIELDS
        for s in range(N - 1, -1, -1):
            if s == 0:
                u = [zero] * FIELDS
            elif s == N - 1:
                u = into[s]
            else:
                u = [into[s][f] + gain[s] * v[f] for f in fields]
            for f in fields:
                rts[half, s, f] = u[f]
                rts[half, s, FIELDS + f] = v[f]
            if s:
                w = [rcv[half, s, 8 + f] + rcv[half, s, 7] * u[f] for f in fields]
                v = w if s == N - 1 else [w[f] + rcv[half, s, 5] * v[f] for f in fields]
        own_backward(half).start()
        for off in range(1, N):
            to = lax.rem(lev + off, N)
            by_slab(to, BACKWARD, lambda part: backward(half, to, part).start())
        return carry

    lax.fori_loop(0, 2, solve, 0)

    def spot(fk, c, r):
        return (fk * 2 + c) * HEIGHT + PAD + r

    def substitute(half):
        own_backward(half).wait()

        def run(part):
            for off in range(1, N):
                backward_from(half, lax.rem(lev + off, N), part).wait_recv()

        by_slab(lev, BACKWARD, run)

        def block(j, carry):
            start = pl.multiple_of(quarter_row(half * 2 + lax.div(j, 2)) + 8 * lax.rem(j, 2), 8)
            rows = pl.ds(start, 8)
            for c in range(2):
                cols = pl.ds(c * LANES, LANES)
                source = solver(lax.div(j, 2), 2 * lax.rem(j, 2) + c)
                x = [None] * FIELDS
                for k in range(LEVELS - 1, -1, -1):
                    e, g = a_v[k, rows, cols], b_v[k, rows, cols]
                    for f in range(FIELDS):
                        u = rtr[half, source, f]
                        beyond = rtr[half, source, FIELDS + f] if k == LEVELS - 1 else x[f]
                        x[f] = m_v[f, k, rows, cols] + g * u + e * beyond
                        at = pl.multiple_of(spot(f * LEVELS + k, c, start), 8)
                        x_v[pl.ds(at, 8), :] = x[f]
            return carry

        lax.fori_loop(0, 4, block, 0)

    def halo(way):
        to = right if way == 0 else left
        return pltpu.make_async_remote_copy(
            src_ref=hs.at[way], dst_ref=hr.at[way], send_sem=hss.at[way], recv_sem=hrs.at[way],
            device_id=(to, lev), device_id_type=MESH)

    def every(c, r):
        return pl.ds(spot(0, c, r), STACK, stride=2 * HEIGHT)

    substitute(0)
    for way, r in ((0, ROWS - 1), (1, 0)):
        for c in range(2):
            weight = s_v[way, r:r + 1, c * LANES:(c + 1) * LANES]
            hs[way, c] = x_v[every(c, r), :] * weight
        halo(way).start()
    substitute(1)
    lane16 = lax.broadcasted_iota(jnp.int32, (QUARTER, LANES), 1)

    def transport(j, carry):
        start = pl.multiple_of(j * QUARTER, QUARTER)
        rows = pl.ds(start, QUARTER)
        co = [[co_v[n, c, rows, :] for c in range(2)] for n in range(5)]

        def one(fk, inner):
            f, k = lax.div(fk, LEVELS), lax.rem(fk, LEVELS)
            at = [pl.multiple_of(spot(fk, c, start), 8) for c in range(2)]
            x = [x_v[pl.ds(at[c], QUARTER), :] for c in range(2)]
            up = [x_v[pl.ds(at[c] - 1, QUARTER), :] for c in range(2)]
            down = [x_v[pl.ds(at[c] + 1, QUARTER), :] for c in range(2)]
            fwd = [pltpu.roll(x[c], 1, 1) for c in range(2)]
            bwd = [pltpu.roll(x[c], LANES - 1, 1) for c in range(2)]
            fwd[1] = jnp.where(lane16 == 0, fwd[0], fwd[1])
            bwd[0] = jnp.where(lane16 == LANES - 1, bwd[1], bwd[0])
            for c in range(2):
                total = x[c] * co[0][c] + up[c] * co[1][c] + down[c] * co[2][c]
                total = total + fwd[c] * co[3][c] + bwd[c] * co[4][c]
                out[f, k, rows, pl.ds(c * LANES, LANES)] = total
            return inner

        return lax.fori_loop(0, STACK, one, carry, unroll=44)

    lax.fori_loop(1, ROWS // QUARTER - 1, transport, 0)
    for way, r in ((0, -1), (1, ROWS)):
        halo(way).wait()
        for c in range(2):
            x_v[every(c, r), :] = hr[way, c]
    lax.fori_loop(0, 2, lambda j, carry: transport(j * (ROWS // QUARTER - 1), carry), 0)

    def drain(part):
        for half in range(2):
            for off in range(1, N):
                forward(half, lax.rem(lev + off, N), part).wait_send()

    by_slab(lev, FORWARD, drain)
    for half in range(2):
        for off in range(1, N):
            to = lax.rem(lev + off, N)
            by_slab(to, BACKWARD, lambda part: backward(half, to, part).wait_send())


def per_device(adjoint_state, lower_coef, upper_coef, stencil_coef, land_mask):
    f32 = jnp.float32
    dma = pltpu.SemaphoreType.DMA
    return pl.pallas_call(
        kernel,
        out_shape=pltpu.VMEM(adjoint_state.shape, f32),
        in_specs=[pl.BlockSpec(memory_space=pltpu.HBM)] * 5,
        out_specs=pl.BlockSpec(memory_space=pltpu.VMEM),
        scratch_shapes=[
            pltpu.VMEM((FIELDS, LEVELS, ROWS, COLS), f32),
            pltpu.VMEM((LEVELS, ROWS, COLS), f32),
            pltpu.VMEM((LEVELS, ROWS, COLS), f32),
            pltpu.VMEM((4, ROWS, COLS), f32),
            pltpu.VMEM((ROWS, COLS), jnp.int32),
            pltpu.VMEM((5, 2, ROWS, LANES), f32),
            pltpu.VMEM((STACK * 2 * HEIGHT, LANES), f32),
            pltpu.VMEM((2, N, PLANES, 8, LANES), f32),
            pltpu.VMEM((2, N, PLANES, 8, LANES), f32),
            pltpu.VMEM((2, N, BACK, 8, LANES), f32),
            pltpu.VMEM((2, N, BACK, 8, LANES), f32),
            pltpu.VMEM((2, 2, STACK, LANES), f32),
            pltpu.VMEM((2, 2, STACK, LANES), f32),
            dma((4, 3)),
            dma((2,)),
            dma((2, N)),
            dma((2, N)),
            dma((2,)),
            dma((2, N)),
            dma((2, N)),
            dma((2,)),
            dma((2,)),
            dma((2,)),
        ],
        compiler_params=pltpu.CompilerParams(
            collective_id=0, has_side_effects=True, vmem_limit_bytes=40 * 2**20),
    )(*(pltpu.with_memory_space_constraint(x, pltpu.HBM) for x in (
        adjoint_state, lower_coef, upper_coef, stencil_coef, land_mask)))


def solution(mesh):
    return jax.shard_map(
        per_device,
        mesh=mesh,
        in_specs=(
            P(None, "lev", "tile", None),
            P("lev", "tile", None),
            P("lev", "tile", None),
            P(None, "tile", None),
            P("tile", None),
        ),
        out_specs=P(None, "lev", "tile", None),
        check_vma=False,
    )
```

```python
import functools

import jax
import jax.numpy as jnp
from jax import lax
from jax.experimental import pallas as pl
from jax.experimental.pallas import tpu as pltpu
from jax.sharding import PartitionSpec as P

MESH = pl.DeviceIdType.MESH
N = 8
FIELDS = 4
LEVELS = 11
ROWS, COLS = 64, 256
LANES = 128
PAD = 8
HEIGHT = ROWS + 2 * PAD
STACK = FIELDS * LEVELS
QUARTER = 16
PLANES = 4 + 2 * FIELDS
BACK = 2 * FIELDS
FORWARD = (slice(0, 1 + FIELDS), slice(0, PLANES), slice(PLANES - 1 - FIELDS, PLANES))
BACKWARD = (slice(FIELDS, BACK), slice(0, BACK), slice(0, FIELDS))


def quarter_row(i):
    return pl.multiple_of(QUARTER * lax.rem(3 * i, 4), QUARTER)


def solver(group, j):
    return 2 * j + lax.rem(group + j, 2)


def spot(fk, c, r):
    return (fk * 2 + c) * HEIGHT + PAD + r


def transport(x_v, co_v, out, start, to):
    start, to = pl.multiple_of(start, QUARTER), pl.multiple_of(to, QUARTER)
    lane = lax.broadcasted_iota(jnp.int32, (QUARTER, LANES), 1)
    co = [[co_v[n, c, pl.ds(start, QUARTER), :] for c in range(2)] for n in range(5)]

    def one(fk, carry):
        f, k = lax.div(fk, LEVELS), lax.rem(fk, LEVELS)
        at = [pl.multiple_of(spot(fk, c, start), 8) for c in range(2)]
        x = [x_v[pl.ds(at[c], QUARTER), :] for c in range(2)]
        up = [x_v[pl.ds(at[c] - 1, QUARTER), :] for c in range(2)]
        down = [x_v[pl.ds(at[c] + 1, QUARTER), :] for c in range(2)]
        fwd = [pltpu.roll(x[c], 1, 1) for c in range(2)]
        bwd = [pltpu.roll(x[c], LANES - 1, 1) for c in range(2)]
        fwd[1] = jnp.where(lane == 0, fwd[0], fwd[1])
        bwd[0] = jnp.where(lane == LANES - 1, bwd[1], bwd[0])
        for c in range(2):
            total = x[c] * co[0][c] + up[c] * co[1][c] + down[c] * co[2][c]
            total = total + fwd[c] * co[3][c] + bwd[c] * co[4][c]
            out[f, k, pl.ds(to, QUARTER), pl.ds(c * LANES, LANES)] = total
        return carry

    return lax.fori_loop(0, STACK, one, 0, unroll=STACK)


def finish(x_v, co_v, hr, part, out, o_v, sem):
    def store(ref, start, to, n):
        return pltpu.make_async_copy(
            ref.at[:, :, pl.ds(start, QUARTER), :], out.at[:, :, pl.ds(to, QUARTER), :], sem.at[n])

    last = ROWS - QUARTER
    copies = [store(part, 2 * QUARTER, QUARTER, 0), store(o_v, 0, 0, 1), store(o_v, last, last, 2),
              store(o_v, 2 * QUARTER, 2 * QUARTER, 3)]
    copies[0].start()
    row = lax.broadcasted_iota(jnp.int32, (8, LANES), 0)
    for n, (start, to, rows) in enumerate(((0, 0, (None, QUARTER)), (QUARTER, last, (last - 1, None)))):
        weight = [[jnp.where(row == r, co_v[1 + i, c, pl.ds(to + 8 * i, 8), :], 0.0) for c in range(2)]
                  for i, r in ((0, 0), (1, 7))]

        def patch(fk, carry):
            f, k = lax.div(fk, LEVELS), lax.rem(fk, LEVELS)
            for c in range(2):
                cols = pl.ds(c * LANES, LANES)
                for i in range(2):
                    if rows[i] is None:
                        term = hr[i, c, pl.ds(fk, 1), :]
                    else:
                        term = x_v[pl.ds(spot(fk, c, rows[i]), 1), :]
                    o_v[f, k, pl.ds(to + 8 * i, 8), cols] = part[f, k, pl.ds(start + 8 * i, 8), cols] + weight[i][c] * term
            return carry

        lax.fori_loop(0, STACK, patch, 0, unroll=STACK)
        copies[1 + n].start()
    transport(x_v, co_v, o_v, 2 * QUARTER, 2 * QUARTER)
    copies[3].start()
    for copy in copies:
        copy.wait()


def kernel(
    adj, low, upp, sten, mask, x_v, co_v, hr, part,
    m_v, a_v, b_v, s_v, k_v, snd, rcv, rts, rtr, hs,
    load_sem, small_sem, fs, fr, fl, bs, br, bl, hss, hrs,
):
    tile = lax.axis_index("tile")
    lev = lax.axis_index("lev")
    tiles = lax.axis_size("tile")

    barrier = pltpu.get_barrier_semaphore()
    for off in range(1, N):
        pl.semaphore_signal(barrier, inc=1, device_id=(tile, lax.rem(lev + off, N)), device_id_type=MESH)
    right, left = lax.rem(tile + 1, tiles), lax.rem(tile + tiles - 1, tiles)
    for t in (right, left):
        pl.semaphore_signal(barrier, inc=1, device_id=(t, lev), device_id_type=MESH)

    def loads(i):
        rows = pl.ds(quarter_row(i), QUARTER)
        return (
            pltpu.make_async_copy(adj.at[:, :, rows, :], m_v.at[:, :, rows, :], load_sem.at[i, 0]),
            pltpu.make_async_copy(low.at[:, rows, :], a_v.at[:, rows, :], load_sem.at[i, 1]),
            pltpu.make_async_copy(upp.at[:, rows, :], b_v.at[:, rows, :], load_sem.at[i, 2]),
        )

    load_mask = pltpu.make_async_copy(mask, k_v, small_sem.at[0])
    load_sten = pltpu.make_async_copy(sten, s_v, small_sem.at[1])
    load_mask.start()
    for i in range(4):
        for c in loads(i):
            c.start()
    load_sten.start()

    @pl.when(lev == 0)
    def _():
        rtr[:, :, :FIELDS] = jnp.zeros((2, N, FIELDS, 8, LANES), jnp.float32)

    @pl.when(lev == N - 1)
    def _():
        rtr[:, :, FIELDS:] = jnp.zeros((2, N, FIELDS, 8, LANES), jnp.float32)

    first = jnp.where(lev == 0, 0.0, 1.0)
    last = jnp.where(lev == N - 1, 0.0, 1.0)

    def eliminate(i):
        for c in loads(i):
            c.wait()
        start = quarter_row(i)
        rows = pl.ds(start, QUARTER)
        half, group = lax.div(i, 2), lax.rem(i, 2)
        keep = k_v[rows, :].astype(jnp.float32)
        r = [None] * FIELDS
        p = [None] * FIELDS
        a = a_v[0, rows, :] * first
        chain = a
        inv = g = q = b = None
        for k in range(LEVELS):
            b_next = b_v[k, rows, :]
            if k == LEVELS - 1:
                b_next = b_next * last
            d = 1.0 + a + b_next
            if k:
                d = d - b * a * inv
            inv = pltpu.reciprocal(d, approx=True)
            if k:
                h = b * inv
                g = h * g
                q = q + chain * g
            else:
                g = inv
                q = chain * g
            for f in range(FIELDS):
                m = m_v[f, k, rows, :] * keep
                if k:
                    r[f] = m * inv + h * r[f]
                    p[f] = p[f] + chain * r[f]
                else:
                    r[f] = m * inv
                    p[f] = chain * r[f]
                m_v[f, k, rows, :] = r[f]
            if k < LEVELS - 1:
                a = a_v[k + 1, rows, :]
                e = a * inv
            else:
                e = inv
            chain = chain * e
            a_v[k, rows, :] = e
            b_v[k, rows, :] = g
            b = b_next
        planes = [b * inv] + [b * r[f] for f in range(FIELDS)] + [chain, b * g, q] + p
        for j in range(4):
            row, col = (j // 2) * 8, (j % 2) * LANES
            for n, plane in enumerate(planes):
                snd[half, solver(group, j), n] = plane[row:row + 8, col:col + LANES]

    def forward(half, to, part):
        return pltpu.make_async_remote_copy(
            src_ref=snd.at[half, to, part], dst_ref=rcv.at[half, lev, part], send_sem=fs.at[half, to],
            recv_sem=fr.at[half, lev], device_id=(tile, to), device_id_type=MESH)

    def forward_from(half, source, part):
        return pltpu.make_async_remote_copy(
            src_ref=snd.at[half, source, part], dst_ref=rcv.at[half, source, part], send_sem=fs.at[half, source],
            recv_sem=fr.at[half, source], device_id=(tile, source), device_id_type=MESH)

    def backward(half, to, part):
        return pltpu.make_async_remote_copy(
            src_ref=rts.at[half, to, part], dst_ref=rtr.at[half, lev, part], send_sem=bs.at[half, to],
            recv_sem=br.at[half, lev], device_id=(tile, to), device_id_type=MESH)

    def backward_from(half, source, part):
        return pltpu.make_async_remote_copy(
            src_ref=rts.at[half, source, part], dst_ref=rtr.at[half, source, part], send_sem=bs.at[half, source],
            recv_sem=br.at[half, source], device_id=(tile, source), device_id_type=MESH)

    def own_forward(half):
        return pltpu.make_async_copy(snd.at[half, lev], rcv.at[half, lev], fl.at[half])

    def own_backward(half):
        return pltpu.make_async_copy(rts.at[half, lev], rtr.at[half, lev], bl.at[half])

    def by_slab(s, parts, run):
        pl.when(s == 0)(lambda: run(parts[0]))
        pl.when(s == N - 1)(lambda: run(parts[2]))
        pl.when((s != 0) & (s != N - 1))(lambda: run(parts[1]))

    def send_forward(i):
        half, group = lax.div(i, 2), lax.rem(i, 2)

        def run(part):
            for j in range(4):
                to = solver(group, j)
                pl.when(to != lev)(lambda: forward(half, to, part).start())

        by_slab(lev, FORWARD, run)
        for j in range(4):
            pl.when(solver(group, j) == lev)(lambda: own_forward(half).start())

    def quarter(i, carry):
        eliminate(i)
        pl.when(i == 0)(lambda: pl.semaphore_wait(barrier, N + 1))
        send_forward(i)
        return carry

    load_mask.wait()
    lax.fori_loop(0, 4, quarter, 0)
    load_sten.wait()

    row = lax.broadcasted_iota(jnp.int32, (ROWS, LANES), 0)
    lane = lax.broadcasted_iota(jnp.int32, (ROWS, LANES), 1)
    has_left = jnp.where(tile == 0, 0.0, 1.0)
    has_right = jnp.where(tile == tiles - 1, 0.0, 1.0)
    for c in range(2):
        cols = pl.ds(c * LANES, LANES)
        east, west, north, south = s_v[0, :, cols], s_v[1, :, cols], s_v[2, :, cols], s_v[3, :, cols]
        co_v[0, c] = 1.0 - (east + west + north + south)
        co_v[1, c] = jnp.where(row == 0, has_left, pltpu.roll(east, 1, 0))
        co_v[2, c] = jnp.where(row == ROWS - 1, has_right, pltpu.roll(west, ROWS - 1, 0))
        before = 0.0 if c == 0 else pltpu.roll(s_v[2, :, :LANES], 1, 1)
        after = pltpu.roll(s_v[3, :, LANES:], LANES - 1, 1) if c == 0 else 0.0
        co_v[3, c] = jnp.where(lane == 0, before, pltpu.roll(north, 1, 1))
        co_v[4, c] = jnp.where(lane == LANES - 1, after, pltpu.roll(south, LANES - 1, 1))

    def clear(n, carry):
        for r in (-PAD, QUARTER, ROWS - QUARTER - 8, ROWS):
            x_v[pl.ds(pl.multiple_of(n * HEIGHT + PAD + r, 8), 8), :] = jnp.zeros((8, LANES), jnp.float32)
        return carry

    lax.fori_loop(0, 2 * STACK, clear, 0, unroll=8)

    def solve(half, carry):
        own_forward(half).wait()
        for s in range(N):
            part = FORWARD[0 if s == 0 else 2 if s == N - 1 else 1]
            pl.when(lev != s)(lambda: forward_from(half, s, part).wait_recv())
        fields = range(FIELDS)
        flux = [rcv[half, 0, 1 + f] for f in fields]
        slope = rcv[half, 0, 0]
        into, gain = [None] * N, [None] * N
        for s in range(1, N):
            aa = rcv[half, s, 7]
            inv = pltpu.reciprocal(1.0 - slope * aa, approx=True)
            into[s] = [(flux[f] + slope * rcv[half, s, 8 + f]) * inv for f in fields]
            if s < N - 1:
                dd, bb, cc = rcv[half, s, 0], rcv[half, s, 5], rcv[half, s, 6]
                gain[s] = slope * bb * inv
                flux = [rcv[half, s, 1 + f] + cc * into[s][f] for f in fields]
                slope = dd + cc * gain[s]
        zero = jnp.zeros((8, LANES), jnp.float32)
        v = [zero] * FIELDS
        for s in range(N - 1, -1, -1):
            if s == 0:
                u = [zero] * FIELDS
            elif s == N - 1:
                u = into[s]
            else:
                u = [into[s][f] + gain[s] * v[f] for f in fields]
            for f in fields:
                rts[half, s, f] = u[f]
                rts[half, s, FIELDS + f] = v[f]
            if s:
                w = [rcv[half, s, 8 + f] + rcv[half, s, 7] * u[f] for f in fields]
                v = w if s == N - 1 else [w[f] + rcv[half, s, 5] * v[f] for f in fields]
        own_backward(half).start()
        for off in range(1, N):
            to = lax.rem(lev + off, N)
            by_slab(to, BACKWARD, lambda part: backward(half, to, part).start())
        return carry

    lax.fori_loop(0, 2, solve, 0)

    def returned(half):
        own_backward(half).wait()

        def run(part):
            for off in range(1, N):
                backward_from(half, lax.rem(lev + off, N), part).wait_recv()

        by_slab(lev, BACKWARD, run)

    def substitute(half, j):
        start = pl.multiple_of(quarter_row(half * 2 + lax.div(j, 2)) + 8 * lax.rem(j, 2), 8)
        rows = pl.ds(start, 8)
        for c in range(2):
            cols = pl.ds(c * LANES, LANES)
            source = solver(lax.div(j, 2), 2 * lax.rem(j, 2) + c)
            x = [None] * FIELDS
            for k in range(LEVELS - 1, -1, -1):
                e, g = a_v[k, rows, cols], b_v[k, rows, cols]
                for f in range(FIELDS):
                    u = rtr[half, source, f]
                    beyond = rtr[half, source, FIELDS + f] if k == LEVELS - 1 else x[f]
                    x[f] = m_v[f, k, rows, cols] + g * u + e * beyond
                    x_v[pl.ds(pl.multiple_of(spot(f * LEVELS + k, c, start), 8), 8), :] = x[f]

    def halo(way):
        to = right if way == 0 else left
        return pltpu.make_async_remote_copy(
            src_ref=hs.at[way], dst_ref=hr.at[way], send_sem=hss.at[way], recv_sem=hrs.at[way],
            device_id=(to, lev), device_id_type=MESH)

    def every(c, r):
        return pl.ds(spot(0, c, r), STACK, stride=2 * HEIGHT)

    def blocks(half, first, count, step):
        def body(n, carry):
            substitute(half, first + n * step)
            return carry

        lax.fori_loop(0, count, body, 0, unroll=2)

    returned(0)
    blocks(0, 0, 2, 3)
    for way, r in ((0, ROWS - 1), (1, 0)):
        for c in range(2):
            weight = s_v[way, r:r + 1, c * LANES:(c + 1) * LANES]
            hs[way, c] = x_v[every(c, r), :] * weight
        halo(way).start()
    blocks(0, 1, 2, 1)
    lax.fori_loop(0, 2, lambda j, carry: transport(x_v, co_v, part, j * (ROWS - QUARTER), j * QUARTER), 0)
    returned(1)
    blocks(1, 0, 4, 1)
    transport(x_v, co_v, part, QUARTER, 2 * QUARTER)
    for way in range(2):
        halo(way).wait()

    def drain(part):
        for half in range(2):
            for off in range(1, N):
                forward(half, lax.rem(lev + off, N), part).wait_send()

    by_slab(lev, FORWARD, drain)
    for half in range(2):
        for off in range(1, N):
            to = lax.rem(lev + off, N)
            by_slab(to, BACKWARD, lambda part: backward(half, to, part).wait_send())


def per_device(adjoint_state, lower_coef, upper_coef, stencil_coef, land_mask):
    f32 = jnp.float32
    dma = pltpu.SemaphoreType.DMA
    space = pltpu.VMEM
    fields, slab, rows, cols = adjoint_state.shape
    parts = pl.pallas_call(
        kernel,
        out_shape=[
            space((STACK * 2 * HEIGHT, LANES), f32),
            space((5, 2, ROWS, LANES), f32),
            space((2, 2, STACK, LANES), f32),
            space((fields, slab, 3 * QUARTER, cols), f32),
        ],
        in_specs=[pl.BlockSpec(memory_space=pltpu.HBM)] * 5,
        out_specs=[pl.BlockSpec(memory_space=space)] * 4,
        scratch_shapes=[
            space((FIELDS, LEVELS, ROWS, COLS), f32),
            space((LEVELS, ROWS, COLS), f32),
            space((LEVELS, ROWS, COLS), f32),
            space((4, ROWS, COLS), f32),
            space((ROWS, COLS), jnp.int32),
            space((2, N, PLANES, 8, LANES), f32),
            space((2, N, PLANES, 8, LANES), f32),
            space((2, N, BACK, 8, LANES), f32),
            space((2, N, BACK, 8, LANES), f32),
            space((2, 2, STACK, LANES), f32),
            dma((4, 3)),
            dma((2,)),
            dma((2, N)),
            dma((2, N)),
            dma((2,)),
            dma((2, N)),
            dma((2, N)),
            dma((2,)),
            dma((2,)),
            dma((2,)),
        ],
        compiler_params=pltpu.CompilerParams(
            collective_id=0, has_side_effects=True, vmem_limit_bytes=32 * 2**20),
    )(*(pltpu.with_memory_space_constraint(x, pltpu.HBM) for x in (
        adjoint_state, lower_coef, upper_coef, stencil_coef, land_mask)))
    return pl.pallas_call(
        finish,
        out_shape=jax.ShapeDtypeStruct(adjoint_state.shape, f32),
        in_specs=[pl.BlockSpec(memory_space=space)] * 4,
        out_specs=pl.BlockSpec(memory_space=pltpu.HBM),
        scratch_shapes=[space(adjoint_state.shape, f32), dma((4,))],
        compiler_params=pltpu.CompilerParams(vmem_limit_bytes=16 * 2**20),
    )(*(pltpu.with_memory_space_constraint(x, space) for x in parts))


def solution(mesh):
    return jax.shard_map(
        per_device,
        mesh=mesh,
        in_specs=(
            P(None, "lev", "tile", None),
            P("lev", "tile", None),
            P("lev", "tile", None),
            P(None, "tile", None),
            P("tile", None),
        ),
        out_specs=P(None, "lev", "tile", None),
        check_vma=False,
    )
```

```python
import functools

import jax
import jax.numpy as jnp
from jax import lax
from jax.experimental import pallas as pl
from jax.experimental.pallas import tpu as pltpu
from jax.sharding import PartitionSpec as P

MESH = pl.DeviceIdType.MESH
N = 8
FIELDS = 4
LEVELS = 11
ROWS, COLS = 64, 256
LANES = 128
PAD = 8
HEIGHT = ROWS + 2 * PAD
STACK = FIELDS * LEVELS
QUARTER = 16
PLANES = 4 + 2 * FIELDS
BACK = 2 * FIELDS
FORWARD = (slice(0, 1 + FIELDS), slice(0, PLANES), slice(PLANES - 1 - FIELDS, PLANES))
BACKWARD = (slice(FIELDS, BACK), slice(0, BACK), slice(0, FIELDS))


def quarter_row(i):
    return pl.multiple_of(QUARTER * lax.rem(3 * i, 4), QUARTER)


def solver(group, j):
    return 2 * j + lax.rem(group + j, 2)


def spot(fk, c, r):
    return (fk * 2 + c) * HEIGHT + PAD + r


def transport(x_v, co_v, out, start, to):
    start, to = pl.multiple_of(start, QUARTER), pl.multiple_of(to, QUARTER)
    lane = lax.broadcasted_iota(jnp.int32, (QUARTER, LANES), 1)
    co = [[co_v[n, c, pl.ds(start, QUARTER), :] for c in range(2)] for n in range(5)]

    def one(fk, carry):
        f, k = lax.div(fk, LEVELS), lax.rem(fk, LEVELS)
        at = [pl.multiple_of(spot(fk, c, start), 8) for c in range(2)]
        x = [x_v[pl.ds(at[c], QUARTER), :] for c in range(2)]
        up = [x_v[pl.ds(at[c] - 1, QUARTER), :] for c in range(2)]
        down = [x_v[pl.ds(at[c] + 1, QUARTER), :] for c in range(2)]
        fwd = [pltpu.roll(x[c], 1, 1) for c in range(2)]
        bwd = [pltpu.roll(x[c], LANES - 1, 1) for c in range(2)]
        fwd[1] = jnp.where(lane == 0, fwd[0], fwd[1])
        bwd[0] = jnp.where(lane == LANES - 1, bwd[1], bwd[0])
        for c in range(2):
            total = x[c] * co[0][c] + up[c] * co[1][c] + down[c] * co[2][c]
            total = total + fwd[c] * co[3][c] + bwd[c] * co[4][c]
            out[f, k, pl.ds(to, QUARTER), pl.ds(c * LANES, LANES)] = total
        return carry

    return lax.fori_loop(0, STACK, one, 0, unroll=STACK)


def finish(x_v, co_v, hr, part, out, o_v, sem):
    def store(ref, start, to, n):
        return pltpu.make_async_copy(
            ref.at[:, :, pl.ds(start, QUARTER), :], out.at[:, :, pl.ds(to, QUARTER), :], sem.at[n])

    last = ROWS - QUARTER
    copies = [store(part, 2 * QUARTER, QUARTER, 0), store(o_v, 0, 0, 1), store(o_v, last, last, 2),
              store(o_v, 2 * QUARTER, 2 * QUARTER, 3)]
    copies[0].start()
    row = lax.broadcasted_iota(jnp.int32, (8, LANES), 0)
    for n, (start, to, rows) in enumerate(((0, 0, (None, QUARTER)), (QUARTER, last, (last - 1, None)))):
        weight = [[jnp.where(row == r, co_v[1 + i, c, pl.ds(to + 8 * i, 8), :], 0.0) for c in range(2)]
                  for i, r in ((0, 0), (1, 7))]

        def patch(fk, carry):
            f, k = lax.div(fk, LEVELS), lax.rem(fk, LEVELS)
            for c in range(2):
                cols = pl.ds(c * LANES, LANES)
                for i in range(2):
                    if rows[i] is None:
                        term = hr[i, c, pl.ds(fk, 1), :]
                    else:
                        term = x_v[pl.ds(spot(fk, c, rows[i]), 1), :]
                    o_v[f, k, pl.ds(to + 8 * i, 8), cols] = part[f, k, pl.ds(start + 8 * i, 8), cols] + weight[i][c] * term
            return carry

        lax.fori_loop(0, STACK, patch, 0, unroll=STACK)
        copies[1 + n].start()
    transport(x_v, co_v, o_v, 2 * QUARTER, 2 * QUARTER)
    copies[3].start()
    for copy in copies:
        copy.wait()


def kernel(
    adj, low, upp, sten, mask, x_v, co_v, hr, part,
    m_v, a_v, b_v, s_v, k_v, snd, rcv, rts, rtr, hs,
    load_sem, small_sem, fs, fr, fl, bs, br, bl, hss, hrs,
):
    tile = lax.axis_index("tile")
    lev = lax.axis_index("lev")
    tiles = lax.axis_size("tile")

    barrier = pltpu.get_barrier_semaphore()
    for off in range(1, N):
        pl.semaphore_signal(barrier, inc=1, device_id=(tile, lax.rem(lev + off, N)), device_id_type=MESH)
    right, left = lax.rem(tile + 1, tiles), lax.rem(tile + tiles - 1, tiles)
    for t in (right, left):
        pl.semaphore_signal(barrier, inc=1, device_id=(t, lev), device_id_type=MESH)

    def loads(i):
        rows = pl.ds(quarter_row(i), QUARTER)
        return (
            pltpu.make_async_copy(adj.at[:, :, rows, :], m_v.at[:, :, rows, :], load_sem.at[i, 0]),
            pltpu.make_async_copy(low.at[:, rows, :], a_v.at[:, rows, :], load_sem.at[i, 1]),
            pltpu.make_async_copy(upp.at[:, rows, :], b_v.at[:, rows, :], load_sem.at[i, 2]),
        )

    load_mask = pltpu.make_async_copy(mask, k_v, small_sem.at[0])
    load_sten = pltpu.make_async_copy(sten, s_v, small_sem.at[1])
    load_mask.start()
    for i in range(4):
        for c in loads(i):
            c.start()
    load_sten.start()

    @pl.when(lev == 0)
    def _():
        rtr[:, :, :FIELDS] = jnp.zeros((2, N, FIELDS, 8, LANES), jnp.float32)

    @pl.when(lev == N - 1)
    def _():
        rtr[:, :, FIELDS:] = jnp.zeros((2, N, FIELDS, 8, LANES), jnp.float32)

    first = jnp.where(lev == 0, 0.0, 1.0)
    last = jnp.where(lev == N - 1, 0.0, 1.0)

    def eliminate(i):
        for c in loads(i):
            c.wait()
        start = quarter_row(i)
        rows = pl.ds(start, QUARTER)
        half, group = lax.div(i, 2), lax.rem(i, 2)
        keep = k_v[rows, :].astype(jnp.float32)
        r = [None] * FIELDS
        p = [None] * FIELDS
        a = a_v[0, rows, :] * first
        chain = a
        inv = g = q = b = None
        for k in range(LEVELS):
            b_next = b_v[k, rows, :]
            if k == LEVELS - 1:
                b_next = b_next * last
            d = 1.0 + a + b_next
            if k:
                d = d - b * a * inv
            inv = pltpu.reciprocal(d, approx=True)
            if k:
                h = b * inv
                g = h * g
                q = q + chain * g
            else:
                g = inv
                q = chain * g
            for f in range(FIELDS):
                m = m_v[f, k, rows, :] * keep
                if k:
                    r[f] = m * inv + h * r[f]
                    p[f] = p[f] + chain * r[f]
                else:
                    r[f] = m * inv
                    p[f] = chain * r[f]
                m_v[f, k, rows, :] = r[f]
            if k < LEVELS - 1:
                a = a_v[k + 1, rows, :]
                e = a * inv
            else:
                e = inv
            chain = chain * e
            a_v[k, rows, :] = e
            b_v[k, rows, :] = g
            b = b_next
        planes = [b * inv] + [b * r[f] for f in range(FIELDS)] + [chain, b * g, q] + p
        for j in range(4):
            row, col = (j // 2) * 8, (j % 2) * LANES
            for n, plane in enumerate(planes):
                snd[half, solver(group, j), n] = plane[row:row + 8, col:col + LANES]

    def forward(half, to, part):
        return pltpu.make_async_remote_copy(
            src_ref=snd.at[half, to, part], dst_ref=rcv.at[half, lev, part], send_sem=fs.at[half, to],
            recv_sem=fr.at[half, lev], device_id=(tile, to), device_id_type=MESH)

    def forward_from(half, source, part):
        return pltpu.make_async_remote_copy(
            src_ref=snd.at[half, source, part], dst_ref=rcv.at[half, source, part], send_sem=fs.at[half, source],
            recv_sem=fr.at[half, source], device_id=(tile, source), device_id_type=MESH)

    def backward(half, to, part):
        return pltpu.make_async_remote_copy(
            src_ref=rts.at[half, to, part], dst_ref=rtr.at[half, lev, part], send_sem=bs.at[half, to],
            recv_sem=br.at[half, lev], device_id=(tile, to), device_id_type=MESH)

    def backward_from(half, source, part):
        return pltpu.make_async_remote_copy(
            src_ref=rts.at[half, source, part], dst_ref=rtr.at[half, source, part], send_sem=bs.at[half, source],
            recv_sem=br.at[half, source], device_id=(tile, source), device_id_type=MESH)

    def own_forward(half):
        return pltpu.make_async_copy(snd.at[half, lev], rcv.at[half, lev], fl.at[half])

    def own_backward(half):
        return pltpu.make_async_copy(rts.at[half, lev], rtr.at[half, lev], bl.at[half])

    def by_slab(s, parts, run):
        pl.when(s == 0)(lambda: run(parts[0]))
        pl.when(s == N - 1)(lambda: run(parts[2]))
        pl.when((s != 0) & (s != N - 1))(lambda: run(parts[1]))

    def send_forward(i):
        half, group = lax.div(i, 2), lax.rem(i, 2)

        def run(part):
            for dx, dz in ((2, 1), (1, 1), (3, 1), (0, 1), (2, 0), (1, 0), (3, 0)):
                to = 2 * lax.rem(lax.div(lev, 2) + dx, 4) + lax.rem(lev + dz, 2)
                forward(half, to, part).start()

        by_slab(lev, FORWARD, run)
        own_forward(half).start()

    def quarter(i, carry):
        eliminate(i)
        pl.when(i == 1)(lambda: pl.semaphore_wait(barrier, N + 1))
        pl.when(lax.rem(i, 2) == 1)(lambda: send_forward(i))
        return carry

    load_mask.wait()
    lax.fori_loop(0, 4, quarter, 0)
    load_sten.wait()

    row = lax.broadcasted_iota(jnp.int32, (ROWS, LANES), 0)
    lane = lax.broadcasted_iota(jnp.int32, (ROWS, LANES), 1)
    has_left = jnp.where(tile == 0, 0.0, 1.0)
    has_right = jnp.where(tile == tiles - 1, 0.0, 1.0)
    for c in range(2):
        cols = pl.ds(c * LANES, LANES)
        east, west, north, south = s_v[0, :, cols], s_v[1, :, cols], s_v[2, :, cols], s_v[3, :, cols]
        co_v[0, c] = 1.0 - (east + west + north + south)
        co_v[1, c] = jnp.where(row == 0, has_left, pltpu.roll(east, 1, 0))
        co_v[2, c] = jnp.where(row == ROWS - 1, has_right, pltpu.roll(west, ROWS - 1, 0))
        before = 0.0 if c == 0 else pltpu.roll(s_v[2, :, :LANES], 1, 1)
        after = pltpu.roll(s_v[3, :, LANES:], LANES - 1, 1) if c == 0 else 0.0
        co_v[3, c] = jnp.where(lane == 0, before, pltpu.roll(north, 1, 1))
        co_v[4, c] = jnp.where(lane == LANES - 1, after, pltpu.roll(south, LANES - 1, 1))

    def clear(n, carry):
        for r in (-PAD, QUARTER, ROWS - QUARTER - 8, ROWS):
            x_v[pl.ds(pl.multiple_of(n * HEIGHT + PAD + r, 8), 8), :] = jnp.zeros((8, LANES), jnp.float32)
        return carry

    lax.fori_loop(0, 2 * STACK, clear, 0, unroll=8)

    def solve(half, carry):
        own_forward(half).wait()
        for s in range(N):
            part = FORWARD[0 if s == 0 else 2 if s == N - 1 else 1]
            pl.when(lev != s)(lambda: forward_from(half, s, part).wait_recv())
        fields = range(FIELDS)
        flux = [rcv[half, 0, 1 + f] for f in fields]
        slope = rcv[half, 0, 0]
        into, gain = [None] * N, [None] * N
        for s in range(1, N):
            aa = rcv[half, s, 7]
            inv = pltpu.reciprocal(1.0 - slope * aa, approx=True)
            into[s] = [(flux[f] + slope * rcv[half, s, 8 + f]) * inv for f in fields]
            if s < N - 1:
                dd, bb, cc = rcv[half, s, 0], rcv[half, s, 5], rcv[half, s, 6]
                gain[s] = slope * bb * inv
                flux = [rcv[half, s, 1 + f] + cc * into[s][f] for f in fields]
                slope = dd + cc * gain[s]
        zero = jnp.zeros((8, LANES), jnp.float32)
        v = [zero] * FIELDS
        for s in range(N - 1, -1, -1):
            if s == 0:
                u = [zero] * FIELDS
            elif s == N - 1:
                u = into[s]
            else:
                u = [into[s][f] + gain[s] * v[f] for f in fields]
            for f in fields:
                rts[half, s, f] = u[f]
                rts[half, s, FIELDS + f] = v[f]
            if s:
                w = [rcv[half, s, 8 + f] + rcv[half, s, 7] * u[f] for f in fields]
                v = w if s == N - 1 else [w[f] + rcv[half, s, 5] * v[f] for f in fields]
        own_backward(half).start()
        for dx, dz in ((2, 1), (1, 1), (3, 1), (0, 1), (2, 0), (1, 0), (3, 0)):
            to = 2 * lax.rem(lax.div(lev, 2) + dx, 4) + lax.rem(lev + dz, 2)
            by_slab(to, BACKWARD, lambda part: backward(half, to, part).start())
        return carry

    lax.fori_loop(0, 2, solve, 0)

    def returned(half):
        own_backward(half).wait()

        def run(part):
            for off in range(1, N):
                backward_from(half, lax.rem(lev + off, N), part).wait_recv()

        by_slab(lev, BACKWARD, run)

    def substitute(half, j):
        start = pl.multiple_of(quarter_row(half * 2 + lax.div(j, 2)) + 8 * lax.rem(j, 2), 8)
        rows = pl.ds(start, 8)
        for c in range(2):
            cols = pl.ds(c * LANES, LANES)
            source = solver(lax.div(j, 2), 2 * lax.rem(j, 2) + c)
            x = [None] * FIELDS
            for k in range(LEVELS - 1, -1, -1):
                e, g = a_v[k, rows, cols], b_v[k, rows, cols]
                for f in range(FIELDS):
                    u = rtr[half, source, f]
                    beyond = rtr[half, source, FIELDS + f] if k == LEVELS - 1 else x[f]
                    x[f] = m_v[f, k, rows, cols] + g * u + e * beyond
                    x_v[pl.ds(pl.multiple_of(spot(f * LEVELS + k, c, start), 8), 8), :] = x[f]

    def halo(way):
        to = right if way == 0 else left
        return pltpu.make_async_remote_copy(
            src_ref=hs.at[way], dst_ref=hr.at[way], send_sem=hss.at[way], recv_sem=hrs.at[way],
            device_id=(to, lev), device_id_type=MESH)

    def every(c, r):
        return pl.ds(spot(0, c, r), STACK, stride=2 * HEIGHT)

    def blocks(half, first, count, step):
        def body(n, carry):
            substitute(half, first + n * step)
            return carry

        lax.fori_loop(0, count, body, 0, unroll=2)

    returned(0)
    blocks(0, 0, 2, 3)
    for way, r in ((0, ROWS - 1), (1, 0)):
        for c in range(2):
            weight = s_v[way, r:r + 1, c * LANES:(c + 1) * LANES]
            hs[way, c] = x_v[every(c, r), :] * weight
        halo(way).start()
    blocks(0, 1, 2, 1)
    lax.fori_loop(0, 2, lambda j, carry: transport(x_v, co_v, part, j * (ROWS - QUARTER), j * QUARTER), 0)
    returned(1)
    blocks(1, 0, 4, 1)
    transport(x_v, co_v, part, QUARTER, 2 * QUARTER)
    for way in range(2):
        halo(way).wait()

    def drain(part):
        for half in range(2):
            for off in range(1, N):
                forward(half, lax.rem(lev + off, N), part).wait_send()

    by_slab(lev, FORWARD, drain)
    for half in range(2):
        for off in range(1, N):
            to = lax.rem(lev + off, N)
            by_slab(to, BACKWARD, lambda part: backward(half, to, part).wait_send())


def per_device(adjoint_state, lower_coef, upper_coef, stencil_coef, land_mask):
    f32 = jnp.float32
    dma = pltpu.SemaphoreType.DMA
    space = pltpu.VMEM
    fields, slab, rows, cols = adjoint_state.shape
    parts = pl.pallas_call(
        kernel,
        out_shape=[
            space((STACK * 2 * HEIGHT, LANES), f32),
            space((5, 2, ROWS, LANES), f32),
            space((2, 2, STACK, LANES), f32),
            space((fields, slab, 3 * QUARTER, cols), f32),
        ],
        in_specs=[pl.BlockSpec(memory_space=pltpu.HBM)] * 5,
        out_specs=[pl.BlockSpec(memory_space=space)] * 4,
        scratch_shapes=[
            space((FIELDS, LEVELS, ROWS, COLS), f32),
            space((LEVELS, ROWS, COLS), f32),
            space((LEVELS, ROWS, COLS), f32),
            space((4, ROWS, COLS), f32),
            space((ROWS, COLS), jnp.int32),
            space((2, N, PLANES, 8, LANES), f32),
            space((2, N, PLANES, 8, LANES), f32),
            space((2, N, BACK, 8, LANES), f32),
            space((2, N, BACK, 8, LANES), f32),
            space((2, 2, STACK, LANES), f32),
            dma((4, 3)),
            dma((2,)),
            dma((2, N)),
            dma((2, N)),
            dma((2,)),
            dma((2, N)),
            dma((2, N)),
            dma((2,)),
            dma((2,)),
            dma((2,)),
        ],
        compiler_params=pltpu.CompilerParams(
            collective_id=0, has_side_effects=True, vmem_limit_bytes=32 * 2**20),
    )(*(pltpu.with_memory_space_constraint(x, pltpu.HBM) for x in (
        adjoint_state, lower_coef, upper_coef, stencil_coef, land_mask)))
    return pl.pallas_call(
        finish,
        out_shape=jax.ShapeDtypeStruct(adjoint_state.shape, f32),
        in_specs=[pl.BlockSpec(memory_space=space)] * 4,
        out_specs=pl.BlockSpec(memory_space=pltpu.HBM),
        scratch_shapes=[space(adjoint_state.shape, f32), dma((4,))],
        compiler_params=pltpu.CompilerParams(vmem_limit_bytes=16 * 2**20),
    )(*(pltpu.with_memory_space_constraint(x, space) for x in parts))


def solution(mesh):
    return jax.shard_map(
        per_device,
        mesh=mesh,
        in_specs=(
            P(None, "lev", "tile", None),
            P("lev", "tile", None),
            P("lev", "tile", None),
            P(None, "tile", None),
            P("tile", None),
        ),
        out_specs=P(None, "lev", "tile", None),
        check_vma=False,
    )
```

```python
import functools

import jax
import jax.numpy as jnp
from jax import lax
from jax.experimental import pallas as pl
from jax.experimental.pallas import tpu as pltpu
from jax.sharding import PartitionSpec as P

MESH = pl.DeviceIdType.MESH
N = 8
FIELDS = 4
LEVELS = 11
ROWS, COLS = 64, 256
LANES = 128
PAD = 8
HEIGHT = ROWS + 2 * PAD
STACK = FIELDS * LEVELS
QUARTER = 16
PLANES = 4 + 2 * FIELDS
BACK = 2 * FIELDS
FORWARD = (slice(0, 1 + FIELDS), slice(0, PLANES), slice(PLANES - 1 - FIELDS, PLANES))
BACKWARD = (slice(FIELDS, BACK), slice(0, BACK), slice(0, FIELDS))


def quarter_row(i):
    return pl.multiple_of(QUARTER * lax.rem(3 * i, 4), QUARTER)


def solver(group, j):
    return 2 * j + lax.rem(group + j, 2)


def solver_of(group, j):
    return 2 * j + (group + j) % 2


def spot(fk, c, r):
    return (fk * 2 + c) * HEIGHT + PAD + r


def transport(x_v, co_v, out, start, to):
    start, to = pl.multiple_of(start, QUARTER), pl.multiple_of(to, QUARTER)
    lane = lax.broadcasted_iota(jnp.int32, (QUARTER, LANES), 1)
    co = [[co_v[n, c, pl.ds(start, QUARTER), :] for c in range(2)] for n in range(5)]

    def one(fk, carry):
        f, k = lax.div(fk, LEVELS), lax.rem(fk, LEVELS)
        at = [pl.multiple_of(spot(fk, c, start), 8) for c in range(2)]
        x = [x_v[pl.ds(at[c], QUARTER), :] for c in range(2)]
        up = [x_v[pl.ds(at[c] - 1, QUARTER), :] for c in range(2)]
        down = [x_v[pl.ds(at[c] + 1, QUARTER), :] for c in range(2)]
        fwd = [pltpu.roll(x[c], 1, 1) for c in range(2)]
        bwd = [pltpu.roll(x[c], LANES - 1, 1) for c in range(2)]
        fwd[1] = jnp.where(lane == 0, fwd[0], fwd[1])
        bwd[0] = jnp.where(lane == LANES - 1, bwd[1], bwd[0])
        for c in range(2):
            total = x[c] * co[0][c] + up[c] * co[1][c] + down[c] * co[2][c]
            total = total + fwd[c] * co[3][c] + bwd[c] * co[4][c]
            out[f, k, pl.ds(to, QUARTER), pl.ds(c * LANES, LANES)] = total
        return carry

    return lax.fori_loop(0, STACK, one, 0, unroll=STACK)


def finish(x_v, co_v, hr, part, out, o_v, sem):
    def store(ref, start, to, n):
        return pltpu.make_async_copy(
            ref.at[:, :, pl.ds(start, QUARTER), :], out.at[:, :, pl.ds(to, QUARTER), :], sem.at[n])

    last = ROWS - QUARTER
    copies = [store(part, 2 * QUARTER, QUARTER, 0), store(o_v, 0, 0, 1), store(o_v, last, last, 2),
              store(o_v, 2 * QUARTER, 2 * QUARTER, 3)]
    copies[0].start()
    row = lax.broadcasted_iota(jnp.int32, (8, LANES), 0)
    for n, (start, to, rows) in enumerate(((0, 0, (None, QUARTER)), (QUARTER, last, (last - 1, None)))):
        weight = [[jnp.where(row == r, co_v[1 + i, c, pl.ds(to + 8 * i, 8), :], 0.0) for c in range(2)]
                  for i, r in ((0, 0), (1, 7))]

        def patch(fk, carry):
            f, k = lax.div(fk, LEVELS), lax.rem(fk, LEVELS)
            for c in range(2):
                cols = pl.ds(c * LANES, LANES)
                for i in range(2):
                    if rows[i] is None:
                        term = hr[i, c, pl.ds(fk, 1), :]
                    else:
                        term = x_v[pl.ds(spot(fk, c, rows[i]), 1), :]
                    o_v[f, k, pl.ds(to + 8 * i, 8), cols] = part[f, k, pl.ds(start + 8 * i, 8), cols] + weight[i][c] * term
            return carry

        lax.fori_loop(0, STACK, patch, 0, unroll=STACK)
        copies[1 + n].start()
    transport(x_v, co_v, o_v, 2 * QUARTER, 2 * QUARTER)
    copies[3].start()
    for copy in copies:
        copy.wait()


def kernel(
    adj, low, upp, sten, mask, x_v, co_v, hr, part,
    m_v, a_v, b_v, s_v, k_v, snd, rcv, rts, rtr, hs,
    load_sem, small_sem, fs, fr, fl, bs, br, bl, hss, hrs,
):
    tile = lax.axis_index("tile")
    lev = lax.axis_index("lev")
    tiles = lax.axis_size("tile")

    barrier = pltpu.get_barrier_semaphore()
    for off in range(1, N):
        pl.semaphore_signal(barrier, inc=1, device_id=(tile, lax.rem(lev + off, N)), device_id_type=MESH)
    right, left = lax.rem(tile + 1, tiles), lax.rem(tile + tiles - 1, tiles)
    for t in (right, left):
        pl.semaphore_signal(barrier, inc=1, device_id=(t, lev), device_id_type=MESH)

    has_previous, has_next = tile != 0, tile != tiles - 1
    for way, has in ((0, has_previous), (1, has_next)):
        @pl.when(jnp.logical_not(has))
        def _():
            hr[way] = jnp.zeros((2, STACK, LANES), jnp.float32)

    def loads(i):
        rows = pl.ds(quarter_row(i), QUARTER)
        return (
            pltpu.make_async_copy(adj.at[:, :, rows, :], m_v.at[:, :, rows, :], load_sem.at[i, 0]),
            pltpu.make_async_copy(low.at[:, rows, :], a_v.at[:, rows, :], load_sem.at[i, 1]),
            pltpu.make_async_copy(upp.at[:, rows, :], b_v.at[:, rows, :], load_sem.at[i, 2]),
        )

    load_mask = pltpu.make_async_copy(mask, k_v, small_sem.at[0])
    load_sten = pltpu.make_async_copy(sten, s_v, small_sem.at[1])
    load_mask.start()
    for i in range(4):
        for c in loads(i):
            c.start()
    load_sten.start()

    @pl.when(lev == 0)
    def _():
        rtr[:, :, :FIELDS] = jnp.zeros((2, N, FIELDS, 8, LANES), jnp.float32)

    @pl.when(lev == N - 1)
    def _():
        rtr[:, :, FIELDS:] = jnp.zeros((2, N, FIELDS, 8, LANES), jnp.float32)

    first = jnp.where(lev == 0, 0.0, 1.0)
    last = jnp.where(lev == N - 1, 0.0, 1.0)

    def eliminate(i):
        for c in loads(i):
            c.wait()
        start = quarter_row(i)
        rows = pl.ds(start, QUARTER)
        half, group = lax.div(i, 2), lax.rem(i, 2)
        keep = k_v[rows, :].astype(jnp.float32)
        r = [None] * FIELDS
        p = [None] * FIELDS
        a = a_v[0, rows, :] * first
        chain = a
        inv = g = q = b = None
        for k in range(LEVELS):
            b_next = b_v[k, rows, :]
            if k == LEVELS - 1:
                b_next = b_next * last
            d = 1.0 + a + b_next
            if k:
                d = d - b * a * inv
            inv = pltpu.reciprocal(d, approx=True)
            if k:
                h = b * inv
                g = h * g
                q = q + chain * g
            else:
                g = inv
                q = chain * g
            for f in range(FIELDS):
                m = m_v[f, k, rows, :] * keep
                if k:
                    r[f] = m * inv + h * r[f]
                    p[f] = p[f] + chain * r[f]
                else:
                    r[f] = m * inv
                    p[f] = chain * r[f]
                m_v[f, k, rows, :] = r[f]
            if k < LEVELS - 1:
                a = a_v[k + 1, rows, :]
                e = a * inv
            else:
                e = inv
            chain = chain * e
            a_v[k, rows, :] = e
            b_v[k, rows, :] = g
            b = b_next
        planes = [b * inv] + [b * r[f] for f in range(FIELDS)] + [chain, b * g, q] + p
        for j in range(4):
            row, col = (j // 2) * 8, (j % 2) * LANES
            for n, plane in enumerate(planes):
                snd[half, solver(group, j), n] = plane[row:row + 8, col:col + LANES]

    def forward(half, to, part):
        return pltpu.make_async_remote_copy(
            src_ref=snd.at[half, to, part], dst_ref=rcv.at[half, lev, part], send_sem=fs.at[half, to],
            recv_sem=fr.at[half, lev], device_id=(tile, to), device_id_type=MESH)

    def forward_from(half, source, part):
        return pltpu.make_async_remote_copy(
            src_ref=snd.at[half, source, part], dst_ref=rcv.at[half, source, part], send_sem=fs.at[half, source],
            recv_sem=fr.at[half, source], device_id=(tile, source), device_id_type=MESH)

    def backward(half, to, part):
        return pltpu.make_async_remote_copy(
            src_ref=rts.at[half, to, part], dst_ref=rtr.at[half, lev, part], send_sem=bs.at[half, to],
            recv_sem=br.at[half, lev], device_id=(tile, to), device_id_type=MESH)

    def backward_from(half, source, part):
        return pltpu.make_async_remote_copy(
            src_ref=rts.at[half, source, part], dst_ref=rtr.at[half, source, part], send_sem=bs.at[half, source],
            recv_sem=br.at[half, source], device_id=(tile, source), device_id_type=MESH)

    def own_forward(half):
        return pltpu.make_async_copy(snd.at[half, lev], rcv.at[half, lev], fl.at[half])

    def own_backward(half):
        return pltpu.make_async_copy(rts.at[half, lev], rtr.at[half, lev], bl.at[half])

    def by_slab(s, parts, run):
        pl.when(s == 0)(lambda: run(parts[0]))
        pl.when(s == N - 1)(lambda: run(parts[2]))
        pl.when((s != 0) & (s != N - 1))(lambda: run(parts[1]))

    def send_forward(i):
        half, group = lax.div(i, 2), lax.rem(i, 2)

        def run(part):
            for dx, dz in ((2, 1), (1, 1), (3, 1), (0, 1), (2, 0), (1, 0), (3, 0)):
                to = 2 * lax.rem(lax.div(lev, 2) + dx, 4) + lax.rem(lev + dz, 2)
                forward(half, to, part).start()

        by_slab(lev, FORWARD, run)
        own_forward(half).start()

    def quarter(i, carry):
        eliminate(i)
        pl.when(i == 1)(lambda: pl.semaphore_wait(barrier, N + 1))
        pl.when(lax.rem(i, 2) == 1)(lambda: send_forward(i))
        return carry

    load_mask.wait()
    lax.fori_loop(0, 4, quarter, 0)
    load_sten.wait()

    row = lax.broadcasted_iota(jnp.int32, (ROWS, LANES), 0)
    lane = lax.broadcasted_iota(jnp.int32, (ROWS, LANES), 1)
    has_left = jnp.where(tile == 0, 0.0, 1.0)
    has_right = jnp.where(tile == tiles - 1, 0.0, 1.0)
    for c in range(2):
        cols = pl.ds(c * LANES, LANES)
        east, west, north, south = s_v[0, :, cols], s_v[1, :, cols], s_v[2, :, cols], s_v[3, :, cols]
        co_v[0, c] = 1.0 - (east + west + north + south)
        co_v[1, c] = jnp.where(row == 0, has_left, pltpu.roll(east, 1, 0))
        co_v[2, c] = jnp.where(row == ROWS - 1, has_right, pltpu.roll(west, ROWS - 1, 0))
        before = 0.0 if c == 0 else pltpu.roll(s_v[2, :, :LANES], 1, 1)
        after = pltpu.roll(s_v[3, :, LANES:], LANES - 1, 1) if c == 0 else 0.0
        co_v[3, c] = jnp.where(lane == 0, before, pltpu.roll(north, 1, 1))
        co_v[4, c] = jnp.where(lane == LANES - 1, after, pltpu.roll(south, LANES - 1, 1))

    def clear(n, carry):
        for r in (-PAD, QUARTER, ROWS - QUARTER - 8, ROWS):
            x_v[pl.ds(pl.multiple_of(n * HEIGHT + PAD + r, 8), 8), :] = jnp.zeros((8, LANES), jnp.float32)
        return carry

    lax.fori_loop(0, 2 * STACK, clear, 0, unroll=8)

    def solve(half, carry):
        own_forward(half).wait()
        for s in range(N):
            part = FORWARD[0 if s == 0 else 2 if s == N - 1 else 1]
            pl.when(lev != s)(lambda: forward_from(half, s, part).wait_recv())
        fields = range(FIELDS)
        flux = [rcv[half, 0, 1 + f] for f in fields]
        slope = rcv[half, 0, 0]
        into, gain = [None] * N, [None] * N
        for s in range(1, N):
            aa = rcv[half, s, 7]
            inv = pltpu.reciprocal(1.0 - slope * aa, approx=True)
            into[s] = [(flux[f] + slope * rcv[half, s, 8 + f]) * inv for f in fields]
            if s < N - 1:
                dd, bb, cc = rcv[half, s, 0], rcv[half, s, 5], rcv[half, s, 6]
                gain[s] = slope * bb * inv
                flux = [rcv[half, s, 1 + f] + cc * into[s][f] for f in fields]
                slope = dd + cc * gain[s]
        zero = jnp.zeros((8, LANES), jnp.float32)
        v = [zero] * FIELDS
        for s in range(N - 1, -1, -1):
            if s == 0:
                u = [zero] * FIELDS
            elif s == N - 1:
                u = into[s]
            else:
                u = [into[s][f] + gain[s] * v[f] for f in fields]
            for f in fields:
                rts[half, s, f] = u[f]
                rts[half, s, FIELDS + f] = v[f]
            if s:
                w = [rcv[half, s, 8 + f] + rcv[half, s, 7] * u[f] for f in fields]
                v = w if s == N - 1 else [w[f] + rcv[half, s, 5] * v[f] for f in fields]
        own_backward(half).start()
        for dx, dz in ((2, 1), (1, 1), (3, 1), (0, 1), (2, 0), (1, 0), (3, 0)):
            to = 2 * lax.rem(lax.div(lev, 2) + dx, 4) + lax.rem(lev + dz, 2)
            by_slab(to, BACKWARD, lambda part: backward(half, to, part).start())
        return carry

    lax.fori_loop(0, 2, solve, 0)

    def returned(half, sources):
        def run(part):
            for s in sources:
                pl.when(lev != s)(lambda: backward_from(half, s, part).wait_recv())

        by_slab(lev, BACKWARD, run)
        for s in sources:
            pl.when(lev == s)(lambda: own_backward(half).wait())

    def substitute(half, j, way=None):
        start = pl.multiple_of(quarter_row(half * 2 + lax.div(j, 2)) + 8 * lax.rem(j, 2), 8)
        rows = pl.ds(start, 8)
        if way is not None:
            edge = 0 if way else ROWS - 1
            weight = [s_v[way, edge:edge + 1, c * LANES:(c + 1) * LANES] for c in range(2)]
        for c in range(2):
            cols = pl.ds(c * LANES, LANES)
            source = solver(lax.div(j, 2), 2 * lax.rem(j, 2) + c)
            x = [None] * FIELDS
            for k in range(LEVELS - 1, -1, -1):
                e, g = a_v[k, rows, cols], b_v[k, rows, cols]
                for f in range(FIELDS):
                    u = rtr[half, source, f]
                    beyond = rtr[half, source, FIELDS + f] if k == LEVELS - 1 else x[f]
                    x[f] = m_v[f, k, rows, cols] + g * u + e * beyond
                    x_v[pl.ds(pl.multiple_of(spot(f * LEVELS + k, c, start), 8), 8), :] = x[f]
                    if way is not None:
                        edge = 0 if way else 7
                        hs[way, c, pl.ds(f * LEVELS + k, 1), :] = x[f][edge:edge + 1, :] * weight[c]

    def halo(way):
        to = right if way == 0 else left
        return pltpu.make_async_remote_copy(
            src_ref=hs.at[way], dst_ref=hr.at[way], send_sem=hss.at[way], recv_sem=hrs.at[way],
            device_id=(to, lev), device_id_type=MESH)

    def blocks(half, first, count, step):
        def body(n, carry):
            substitute(half, first + n * step)
            return carry

        lax.fori_loop(0, count, body, 0, unroll=2)

    for way, j, tiles_of in ((1, 0, (0, 1)), (0, 3, (2, 3))):
        returned(0, [solver_of(j // 2, n) for n in tiles_of])
        substitute(0, j, way)
        has = has_next if way == 0 else has_previous
        pl.when(has)(lambda: halo(way).start())
    returned(0, [solver_of(0, 2), solver_of(0, 3), solver_of(1, 0), solver_of(1, 1)])
    blocks(0, 1, 2, 1)
    lax.fori_loop(0, 2, lambda j, carry: transport(x_v, co_v, part, j * (ROWS - QUARTER), j * QUARTER), 0)
    returned(1, range(N))
    blocks(1, 0, 4, 1)
    transport(x_v, co_v, part, QUARTER, 2 * QUARTER)
    for way in range(2):
        to, of = (has_next, has_previous) if way == 0 else (has_previous, has_next)
        pl.when(of)(lambda: halo(way).wait_recv())
        pl.when(to)(lambda: halo(way).wait_send())

    def drain(part):
        for half in range(2):
            for off in range(1, N):
                forward(half, lax.rem(lev + off, N), part).wait_send()

    by_slab(lev, FORWARD, drain)
    for half in range(2):
        for off in range(1, N):
            to = lax.rem(lev + off, N)
            by_slab(to, BACKWARD, lambda part: backward(half, to, part).wait_send())


def per_device(adjoint_state, lower_coef, upper_coef, stencil_coef, land_mask):
    f32 = jnp.float32
    dma = pltpu.SemaphoreType.DMA
    space = pltpu.VMEM
    fields, slab, rows, cols = adjoint_state.shape
    parts = pl.pallas_call(
        kernel,
        out_shape=[
            space((STACK * 2 * HEIGHT, LANES), f32),
            space((5, 2, ROWS, LANES), f32),
            space((2, 2, STACK, LANES), f32),
            space((fields, slab, 3 * QUARTER, cols), f32),
        ],
        in_specs=[pl.BlockSpec(memory_space=pltpu.HBM)] * 5,
        out_specs=[pl.BlockSpec(memory_space=space)] * 4,
        scratch_shapes=[
            space((FIELDS, LEVELS, ROWS, COLS), f32),
            space((LEVELS, ROWS, COLS), f32),
            space((LEVELS, ROWS, COLS), f32),
            space((4, ROWS, COLS), f32),
            space((ROWS, COLS), jnp.int32),
            space((2, N, PLANES, 8, LANES), f32),
            space((2, N, PLANES, 8, LANES), f32),
            space((2, N, BACK, 8, LANES), f32),
            space((2, N, BACK, 8, LANES), f32),
            space((2, 2, STACK, LANES), f32),
            dma((4, 3)),
            dma((2,)),
            dma((2, N)),
            dma((2, N)),
            dma((2,)),
            dma((2, N)),
            dma((2, N)),
            dma((2,)),
            dma((2,)),
            dma((2,)),
        ],
        compiler_params=pltpu.CompilerParams(
            collective_id=0, has_side_effects=True, vmem_limit_bytes=32 * 2**20),
    )(*(pltpu.with_memory_space_constraint(x, pltpu.HBM) for x in (
        adjoint_state, lower_coef, upper_coef, stencil_coef, land_mask)))
    return pl.pallas_call(
        finish,
        out_shape=jax.ShapeDtypeStruct(adjoint_state.shape, f32),
        in_specs=[pl.BlockSpec(memory_space=space)] * 4,
        out_specs=pl.BlockSpec(memory_space=pltpu.HBM),
        scratch_shapes=[space(adjoint_state.shape, f32), dma((4,))],
        compiler_params=pltpu.CompilerParams(vmem_limit_bytes=16 * 2**20),
    )(*(pltpu.with_memory_space_constraint(x, space) for x in parts))


def solution(mesh):
    return jax.shard_map(
        per_device,
        mesh=mesh,
        in_specs=(
            P(None, "lev", "tile", None),
            P("lev", "tile", None),
            P("lev", "tile", None),
            P(None, "tile", None),
            P("tile", None),
        ),
        out_specs=P(None, "lev", "tile", None),
        check_vma=False,
    )
```

```python
import functools

import jax
import jax.numpy as jnp
from jax import lax
from jax.experimental import pallas as pl
from jax.experimental.pallas import tpu as pltpu
from jax.sharding import PartitionSpec as P

MESH = pl.DeviceIdType.MESH
N = 8
FIELDS = 4
LEVELS = 11
ROWS, COLS = 64, 256
LANES = 128
PAD = 8
HEIGHT = ROWS + 2 * PAD
STACK = FIELDS * LEVELS
QUARTER = 16
PLANES = 4 + 2 * FIELDS
BACK = 2 * FIELDS
FORWARD = (slice(0, 1 + FIELDS), slice(0, PLANES), slice(PLANES - 1 - FIELDS, PLANES))
BACKWARD = (slice(FIELDS, BACK), slice(0, BACK), slice(0, FIELDS))


def quarter_row(i):
    return pl.multiple_of(QUARTER * lax.rem(3 * i, 4), QUARTER)


def solver(group, j):
    return 2 * j + lax.rem(group + j, 2)


def solver_of(group, j):
    return 2 * j + (group + j) % 2


def spot(fk, c, r):
    return (fk * 2 + c) * HEIGHT + PAD + r


def transport(x_v, co_v, out, start, to):
    start, to = pl.multiple_of(start, QUARTER), pl.multiple_of(to, QUARTER)
    lane = lax.broadcasted_iota(jnp.int32, (QUARTER, LANES), 1)
    co = [[co_v[n, c, pl.ds(start, QUARTER), :] for c in range(2)] for n in range(5)]

    def one(fk, carry):
        f, k = lax.div(fk, LEVELS), lax.rem(fk, LEVELS)
        at = [pl.multiple_of(spot(fk, c, start), 8) for c in range(2)]
        x = [x_v[pl.ds(at[c], QUARTER), :] for c in range(2)]
        up = [x_v[pl.ds(at[c] - 1, QUARTER), :] for c in range(2)]
        down = [x_v[pl.ds(at[c] + 1, QUARTER), :] for c in range(2)]
        fwd = [pltpu.roll(x[c], 1, 1) for c in range(2)]
        bwd = [pltpu.roll(x[c], LANES - 1, 1) for c in range(2)]
        fwd[1] = jnp.where(lane == 0, fwd[0], fwd[1])
        bwd[0] = jnp.where(lane == LANES - 1, bwd[1], bwd[0])
        for c in range(2):
            total = x[c] * co[0][c] + up[c] * co[1][c] + down[c] * co[2][c]
            total = total + fwd[c] * co[3][c] + bwd[c] * co[4][c]
            out[f, k, pl.ds(to, QUARTER), pl.ds(c * LANES, LANES)] = total
        return carry

    return lax.fori_loop(0, STACK, one, 0, unroll=STACK)


def finish(x_v, co_v, hr, part, out, o_v, sem):
    def store(ref, start, to, n):
        return pltpu.make_async_copy(
            ref.at[:, :, pl.ds(start, QUARTER), :], out.at[:, :, pl.ds(to, QUARTER), :], sem.at[n])

    last = ROWS - QUARTER
    copies = [store(part, 2 * QUARTER, QUARTER, 0), store(o_v, 0, 0, 1), store(o_v, last, last, 2),
              store(o_v, 2 * QUARTER, 2 * QUARTER, 3)]
    copies[0].start()
    row = lax.broadcasted_iota(jnp.int32, (8, LANES), 0)
    for n, (start, to, rows) in enumerate(((0, 0, (None, QUARTER)), (QUARTER, last, (last - 1, None)))):
        weight = [[jnp.where(row == r, co_v[1 + i, c, pl.ds(to + 8 * i, 8), :], 0.0) for c in range(2)]
                  for i, r in ((0, 0), (1, 7))]

        def patch(fk, carry):
            f, k = lax.div(fk, LEVELS), lax.rem(fk, LEVELS)
            for c in range(2):
                cols = pl.ds(c * LANES, LANES)
                for i in range(2):
                    if rows[i] is None:
                        term = hr[i, c, pl.ds(fk, 1), :]
                    else:
                        term = x_v[pl.ds(spot(fk, c, rows[i]), 1), :]
                    o_v[f, k, pl.ds(to + 8 * i, 8), cols] = part[f, k, pl.ds(start + 8 * i, 8), cols] + weight[i][c] * term
            return carry

        lax.fori_loop(0, STACK, patch, 0, unroll=STACK)
        copies[1 + n].start()
    transport(x_v, co_v, o_v, 2 * QUARTER, 2 * QUARTER)
    copies[3].start()
    for copy in copies:
        copy.wait()


def kernel(
    adj, low, upp, sten, mask, x_v, co_v, hr, part,
    m_v, a_v, b_v, s_v, k_v, snd, rcv, rts, rtr, hs,
    load_sem, small_sem, fs, fr, fl, bs, br, bl, hss, hrs,
):
    tile = lax.axis_index("tile")
    lev = lax.axis_index("lev")
    tiles = lax.axis_size("tile")

    barrier = pltpu.get_barrier_semaphore()
    for off in range(1, N):
        pl.semaphore_signal(barrier, inc=1, device_id=(tile, lax.rem(lev + off, N)), device_id_type=MESH)
    right, left = lax.rem(tile + 1, tiles), lax.rem(tile + tiles - 1, tiles)
    for t in (right, left):
        pl.semaphore_signal(barrier, inc=1, device_id=(t, lev), device_id_type=MESH)

    has_previous, has_next = tile != 0, tile != tiles - 1
    for way, has in ((0, has_previous), (1, has_next)):
        @pl.when(jnp.logical_not(has))
        def _():
            hr[way] = jnp.zeros((2, STACK, LANES), jnp.float32)

    def loads(i):
        rows = pl.ds(quarter_row(i), QUARTER)
        return (
            pltpu.make_async_copy(adj.at[:, :, rows, :], m_v.at[:, :, rows, :], load_sem.at[i, 0]),
            pltpu.make_async_copy(low.at[:, rows, :], a_v.at[:, rows, :], load_sem.at[i, 1]),
            pltpu.make_async_copy(upp.at[:, rows, :], b_v.at[:, rows, :], load_sem.at[i, 2]),
        )

    load_mask = pltpu.make_async_copy(mask, k_v, small_sem.at[0])
    load_sten = pltpu.make_async_copy(sten, s_v, small_sem.at[1])
    load_mask.start()
    for i in range(2):
        for c in loads(i):
            c.start()
    load_sten.start()

    @pl.when(lev == 0)
    def _():
        rtr[:, :, :FIELDS] = jnp.zeros((2, N, FIELDS, 8, LANES), jnp.float32)

    @pl.when(lev == N - 1)
    def _():
        rtr[:, :, FIELDS:] = jnp.zeros((2, N, FIELDS, 8, LANES), jnp.float32)

    first = jnp.where(lev == 0, 0.0, 1.0)
    last = jnp.where(lev == N - 1, 0.0, 1.0)

    def eliminate(i):
        for c in loads(i):
            c.wait()

        @pl.when(i < 2)
        def _():
            for c in loads(i + 2):
                c.start()

        start = quarter_row(i)
        rows = pl.ds(start, QUARTER)
        half, group = lax.div(i, 2), lax.rem(i, 2)
        keep = k_v[rows, :].astype(jnp.float32)
        r = [None] * FIELDS
        p = [None] * FIELDS
        a = a_v[0, rows, :] * first
        chain = a
        inv = g = q = b = None
        for k in range(LEVELS):
            b_next = b_v[k, rows, :]
            if k == LEVELS - 1:
                b_next = b_next * last
            d = 1.0 + a + b_next
            if k:
                d = d - b * a * inv
            inv = pltpu.reciprocal(d, approx=True)
            if k:
                h = b * inv
                g = h * g
                q = q + chain * g
            else:
                g = inv
                q = chain * g
            for f in range(FIELDS):
                m = m_v[f, k, rows, :] * keep
                if k:
                    r[f] = m * inv + h * r[f]
                    p[f] = p[f] + chain * r[f]
                else:
                    r[f] = m * inv
                    p[f] = chain * r[f]
                m_v[f, k, rows, :] = r[f]
            if k < LEVELS - 1:
                a = a_v[k + 1, rows, :]
                e = a * inv
            else:
                e = inv
            chain = chain * e
            a_v[k, rows, :] = e
            b_v[k, rows, :] = g
            b = b_next
        planes = [b * inv] + [b * r[f] for f in range(FIELDS)] + [chain, b * g, q] + p
        for j in range(4):
            row, col = (j // 2) * 8, (j % 2) * LANES
            for n, plane in enumerate(planes):
                snd[half, solver(group, j), n] = plane[row:row + 8, col:col + LANES]

    def forward(half, to, part):
        return pltpu.make_async_remote_copy(
            src_ref=snd.at[half, to, part], dst_ref=rcv.at[half, lev, part], send_sem=fs.at[half, to],
            recv_sem=fr.at[half, lev], device_id=(tile, to), device_id_type=MESH)

    def forward_from(half, source, part):
        return pltpu.make_async_remote_copy(
            src_ref=snd.at[half, source, part], dst_ref=rcv.at[half, source, part], send_sem=fs.at[half, source],
            recv_sem=fr.at[half, source], device_id=(tile, source), device_id_type=MESH)

    def backward(half, to, part):
        return pltpu.make_async_remote_copy(
            src_ref=rts.at[half, to, part], dst_ref=rtr.at[half, lev, part], send_sem=bs.at[half, to],
            recv_sem=br.at[half, lev], device_id=(tile, to), device_id_type=MESH)

    def backward_from(half, source, part):
        return pltpu.make_async_remote_copy(
            src_ref=rts.at[half, source, part], dst_ref=rtr.at[half, source, part], send_sem=bs.at[half, source],
            recv_sem=br.at[half, source], device_id=(tile, source), device_id_type=MESH)

    def own_forward(half):
        return pltpu.make_async_copy(snd.at[half, lev], rcv.at[half, lev], fl.at[half])

    def own_backward(half):
        return pltpu.make_async_copy(rts.at[half, lev], rtr.at[half, lev], bl.at[half])

    def by_slab(s, parts, run):
        pl.when(s == 0)(lambda: run(parts[0]))
        pl.when(s == N - 1)(lambda: run(parts[2]))
        pl.when((s != 0) & (s != N - 1))(lambda: run(parts[1]))

    def send_forward(i):
        half, group = lax.div(i, 2), lax.rem(i, 2)

        def run(part):
            for dx, dz in ((2, 1), (1, 1), (3, 1), (0, 1), (2, 0), (1, 0), (3, 0)):
                to = 2 * lax.rem(lax.div(lev, 2) + dx, 4) + lax.rem(lev + dz, 2)
                forward(half, to, part).start()

        by_slab(lev, FORWARD, run)
        own_forward(half).start()

    def quarter(i, carry):
        eliminate(i)
        pl.when(i == 1)(lambda: pl.semaphore_wait(barrier, N + 1))
        pl.when(lax.rem(i, 2) == 1)(lambda: send_forward(i))
        return carry

    load_mask.wait()
    lax.fori_loop(0, 4, quarter, 0)
    load_sten.wait()

    row = lax.broadcasted_iota(jnp.int32, (ROWS, LANES), 0)
    lane = lax.broadcasted_iota(jnp.int32, (ROWS, LANES), 1)
    has_left = jnp.where(tile == 0, 0.0, 1.0)
    has_right = jnp.where(tile == tiles - 1, 0.0, 1.0)
    for c in range(2):
        cols = pl.ds(c * LANES, LANES)
        east, west, north, south = s_v[0, :, cols], s_v[1, :, cols], s_v[2, :, cols], s_v[3, :, cols]
        co_v[0, c] = 1.0 - (east + west + north + south)
        co_v[1, c] = jnp.where(row == 0, has_left, pltpu.roll(east, 1, 0))
        co_v[2, c] = jnp.where(row == ROWS - 1, has_right, pltpu.roll(west, ROWS - 1, 0))
        before = 0.0 if c == 0 else pltpu.roll(s_v[2, :, :LANES], 1, 1)
        after = pltpu.roll(s_v[3, :, LANES:], LANES - 1, 1) if c == 0 else 0.0
        co_v[3, c] = jnp.where(lane == 0, before, pltpu.roll(north, 1, 1))
        co_v[4, c] = jnp.where(lane == LANES - 1, after, pltpu.roll(south, LANES - 1, 1))

    def clear(n, carry):
        for r in (-PAD, QUARTER, ROWS - QUARTER - 8, ROWS):
            x_v[pl.ds(pl.multiple_of(n * HEIGHT + PAD + r, 8), 8), :] = jnp.zeros((8, LANES), jnp.float32)
        return carry

    lax.fori_loop(0, 2 * STACK, clear, 0, unroll=8)

    def solve(half, carry):
        own_forward(half).wait()
        for s in range(N):
            part = FORWARD[0 if s == 0 else 2 if s == N - 1 else 1]
            pl.when(lev != s)(lambda: forward_from(half, s, part).wait_recv())
        fields = range(FIELDS)
        flux = [rcv[half, 0, 1 + f] for f in fields]
        slope = rcv[half, 0, 0]
        into, gain = [None] * N, [None] * N
        for s in range(1, N):
            aa = rcv[half, s, 7]
            inv = pltpu.reciprocal(1.0 - slope * aa, approx=True)
            into[s] = [(flux[f] + slope * rcv[half, s, 8 + f]) * inv for f in fields]
            if s < N - 1:
                dd, bb, cc = rcv[half, s, 0], rcv[half, s, 5], rcv[half, s, 6]
                gain[s] = slope * bb * inv
                flux = [rcv[half, s, 1 + f] + cc * into[s][f] for f in fields]
                slope = dd + cc * gain[s]
        zero = jnp.zeros((8, LANES), jnp.float32)
        v = [zero] * FIELDS
        for s in range(N - 1, -1, -1):
            if s == 0:
                u = [zero] * FIELDS
            elif s == N - 1:
                u = into[s]
            else:
                u = [into[s][f] + gain[s] * v[f] for f in fields]
            for f in fields:
                rts[half, s, f] = u[f]
                rts[half, s, FIELDS + f] = v[f]
            if s:
                w = [rcv[half, s, 8 + f] + rcv[half, s, 7] * u[f] for f in fields]
                v = w if s == N - 1 else [w[f] + rcv[half, s, 5] * v[f] for f in fields]
        own_backward(half).start()
        for dx, dz in ((2, 1), (1, 1), (3, 1), (0, 1), (2, 0), (1, 0), (3, 0)):
            to = 2 * lax.rem(lax.div(lev, 2) + dx, 4) + lax.rem(lev + dz, 2)
            by_slab(to, BACKWARD, lambda part: backward(half, to, part).start())
        return carry

    lax.fori_loop(0, 2, solve, 0)

    def returned(half, sources):
        def run(part):
            for s in sources:
                pl.when(lev != s)(lambda: backward_from(half, s, part).wait_recv())

        by_slab(lev, BACKWARD, run)
        for s in sources:
            pl.when(lev == s)(lambda: own_backward(half).wait())

    def substitute(half, j, way=None):
        start = pl.multiple_of(quarter_row(half * 2 + lax.div(j, 2)) + 8 * lax.rem(j, 2), 8)
        rows = pl.ds(start, 8)
        if way is not None:
            edge = 0 if way else ROWS - 1
            weight = [s_v[way, edge:edge + 1, c * LANES:(c + 1) * LANES] for c in range(2)]
        for c in range(2):
            cols = pl.ds(c * LANES, LANES)
            source = solver(lax.div(j, 2), 2 * lax.rem(j, 2) + c)
            x = [None] * FIELDS
            for k in range(LEVELS - 1, -1, -1):
                e, g = a_v[k, rows, cols], b_v[k, rows, cols]
                for f in range(FIELDS):
                    u = rtr[half, source, f]
                    beyond = rtr[half, source, FIELDS + f] if k == LEVELS - 1 else x[f]
                    x[f] = m_v[f, k, rows, cols] + g * u + e * beyond
                    x_v[pl.ds(pl.multiple_of(spot(f * LEVELS + k, c, start), 8), 8), :] = x[f]
                    if way is not None:
                        edge = 0 if way else 7
                        hs[way, c, pl.ds(f * LEVELS + k, 1), :] = x[f][edge:edge + 1, :] * weight[c]

    def halo(way):
        to = right if way == 0 else left
        return pltpu.make_async_remote_copy(
            src_ref=hs.at[way], dst_ref=hr.at[way], send_sem=hss.at[way], recv_sem=hrs.at[way],
            device_id=(to, lev), device_id_type=MESH)

    def blocks(half, first, count, step):
        def body(n, carry):
            substitute(half, first + n * step)
            return carry

        lax.fori_loop(0, count, body, 0, unroll=2)

    for way, j, tiles_of in ((1, 0, (0, 1)), (0, 3, (2, 3))):
        returned(0, [solver_of(j // 2, n) for n in tiles_of])
        substitute(0, j, way)
        has = has_next if way == 0 else has_previous
        pl.when(has)(lambda: halo(way).start())
    returned(0, [solver_of(0, 2), solver_of(0, 3), solver_of(1, 0), solver_of(1, 1)])
    blocks(0, 1, 2, 1)
    lax.fori_loop(0, 2, lambda j, carry: transport(x_v, co_v, part, j * (ROWS - QUARTER), j * QUARTER), 0)
    returned(1, range(N))
    blocks(1, 0, 4, 1)
    transport(x_v, co_v, part, QUARTER, 2 * QUARTER)
    for way in range(2):
        to, of = (has_next, has_previous) if way == 0 else (has_previous, has_next)
        pl.when(of)(lambda: halo(way).wait_recv())
        pl.when(to)(lambda: halo(way).wait_send())

    def drain(part):
        for half in range(2):
            for off in range(1, N):
                forward(half, lax.rem(lev + off, N), part).wait_send()

    by_slab(lev, FORWARD, drain)
    for half in range(2):
        for off in range(1, N):
            to = lax.rem(lev + off, N)
            by_slab(to, BACKWARD, lambda part: backward(half, to, part).wait_send())


def per_device(adjoint_state, lower_coef, upper_coef, stencil_coef, land_mask):
    f32 = jnp.float32
    dma = pltpu.SemaphoreType.DMA
    space = pltpu.VMEM
    fields, slab, rows, cols = adjoint_state.shape
    parts = pl.pallas_call(
        kernel,
        out_shape=[
            space((STACK * 2 * HEIGHT, LANES), f32),
            space((5, 2, ROWS, LANES), f32),
            space((2, 2, STACK, LANES), f32),
            space((fields, slab, 3 * QUARTER, cols), f32),
        ],
        in_specs=[pl.BlockSpec(memory_space=pltpu.HBM)] * 5,
        out_specs=[pl.BlockSpec(memory_space=space)] * 4,
        scratch_shapes=[
            space((FIELDS, LEVELS, ROWS, COLS), f32),
            space((LEVELS, ROWS, COLS), f32),
            space((LEVELS, ROWS, COLS), f32),
            space((4, ROWS, COLS), f32),
            space((ROWS, COLS), jnp.int32),
            space((2, N, PLANES, 8, LANES), f32),
            space((2, N, PLANES, 8, LANES), f32),
            space((2, N, BACK, 8, LANES), f32),
            space((2, N, BACK, 8, LANES), f32),
            space((2, 2, STACK, LANES), f32),
            dma((4, 3)),
            dma((2,)),
            dma((2, N)),
            dma((2, N)),
            dma((2,)),
            dma((2, N)),
            dma((2, N)),
            dma((2,)),
            dma((2,)),
            dma((2,)),
        ],
        compiler_params=pltpu.CompilerParams(
            collective_id=0, has_side_effects=True, vmem_limit_bytes=32 * 2**20),
    )(*(pltpu.with_memory_space_constraint(x, pltpu.HBM) for x in (
        adjoint_state, lower_coef, upper_coef, stencil_coef, land_mask)))
    return pl.pallas_call(
        finish,
        out_shape=jax.ShapeDtypeStruct(adjoint_state.shape, f32),
        in_specs=[pl.BlockSpec(memory_space=space)] * 4,
        out_specs=pl.BlockSpec(memory_space=pltpu.HBM),
        scratch_shapes=[space(adjoint_state.shape, f32), dma((4,))],
        compiler_params=pltpu.CompilerParams(vmem_limit_bytes=16 * 2**20),
    )(*(pltpu.with_memory_space_constraint(x, space) for x in parts))


def solution(mesh):
    return jax.shard_map(
        per_device,
        mesh=mesh,
        in_specs=(
            P(None, "lev", "tile", None),
            P("lev", "tile", None),
            P("lev", "tile", None),
            P(None, "tile", None),
            P("tile", None),
        ),
        out_specs=P(None, "lev", "tile", None),
        check_vma=False,
    )
```

```python
import functools

import jax
import jax.numpy as jnp
from jax import lax
from jax.experimental import pallas as pl
from jax.experimental.pallas import tpu as pltpu
from jax.sharding import PartitionSpec as P

MESH = pl.DeviceIdType.MESH
N = 8
FIELDS = 4
LEVELS = 11
ROWS, COLS = 64, 256
LANES = 128
PAD = 8
HEIGHT = ROWS + 2 * PAD
STACK = FIELDS * LEVELS
QUARTER = 16
PLANES = 4 + 2 * FIELDS
BACK = 2 * FIELDS
FORWARD = (slice(0, 1 + FIELDS), slice(0, PLANES), slice(PLANES - 1 - FIELDS, PLANES))
BACKWARD = (slice(FIELDS, BACK), slice(0, BACK), slice(0, FIELDS))


def quarter_row(i):
    return pl.multiple_of(QUARTER * lax.rem(3 * i, 4), QUARTER)


def solver(group, j):
    return 2 * j + lax.rem(group + j, 2)


def solver_of(group, j):
    return 2 * j + (group + j) % 2


def spot(fk, c, r):
    return (fk * 2 + c) * HEIGHT + PAD + r


def transport(x_v, co_v, out, start, to):
    start, to = pl.multiple_of(start, QUARTER), pl.multiple_of(to, QUARTER)
    lane = lax.broadcasted_iota(jnp.int32, (QUARTER, LANES), 1)
    co = [[co_v[n, c, pl.ds(start, QUARTER), :] for c in range(2)] for n in range(5)]

    def one(fk, carry):
        f, k = lax.div(fk, LEVELS), lax.rem(fk, LEVELS)
        at = [pl.multiple_of(spot(fk, c, start), 8) for c in range(2)]
        x = [x_v[pl.ds(at[c], QUARTER), :] for c in range(2)]
        up = [x_v[pl.ds(at[c] - 1, QUARTER), :] for c in range(2)]
        down = [x_v[pl.ds(at[c] + 1, QUARTER), :] for c in range(2)]
        fwd = [pltpu.roll(x[c], 1, 1) for c in range(2)]
        bwd = [pltpu.roll(x[c], LANES - 1, 1) for c in range(2)]
        fwd[1] = jnp.where(lane == 0, fwd[0], fwd[1])
        bwd[0] = jnp.where(lane == LANES - 1, bwd[1], bwd[0])
        for c in range(2):
            total = x[c] * co[0][c] + up[c] * co[1][c] + down[c] * co[2][c]
            total = total + fwd[c] * co[3][c] + bwd[c] * co[4][c]
            out[f, k, pl.ds(to, QUARTER), pl.ds(c * LANES, LANES)] = total
        return carry

    return lax.fori_loop(0, STACK, one, 0, unroll=STACK)


def finish(x_v, co_v, hr, part, out, o_v, sem):
    def store(ref, start, to, n):
        return pltpu.make_async_copy(
            ref.at[:, :, pl.ds(start, QUARTER), :], out.at[:, :, pl.ds(to, QUARTER), :], sem.at[n])

    last = ROWS - QUARTER
    copies = [store(part, 2 * QUARTER, QUARTER, 0), store(o_v, 0, 0, 1), store(o_v, last, last, 2),
              store(o_v, 2 * QUARTER, 2 * QUARTER, 3)]
    copies[0].start()
    row = lax.broadcasted_iota(jnp.int32, (8, LANES), 0)
    for n, (start, to, rows) in enumerate(((0, 0, (None, QUARTER)), (QUARTER, last, (last - 1, None)))):
        weight = [[jnp.where(row == r, co_v[1 + i, c, pl.ds(to + 8 * i, 8), :], 0.0) for c in range(2)]
                  for i, r in ((0, 0), (1, 7))]

        def patch(fk, carry):
            f, k = lax.div(fk, LEVELS), lax.rem(fk, LEVELS)
            for c in range(2):
                cols = pl.ds(c * LANES, LANES)
                for i in range(2):
                    if rows[i] is None:
                        term = hr[i, c, pl.ds(fk, 1), :]
                    else:
                        term = x_v[pl.ds(spot(fk, c, rows[i]), 1), :]
                    o_v[f, k, pl.ds(to + 8 * i, 8), cols] = part[f, k, pl.ds(start + 8 * i, 8), cols] + weight[i][c] * term
            return carry

        lax.fori_loop(0, STACK, patch, 0, unroll=STACK)
        copies[1 + n].start()
    transport(x_v, co_v, o_v, 2 * QUARTER, 2 * QUARTER)
    copies[3].start()
    for copy in copies:
        copy.wait()


def kernel(
    adj, low, upp, sten, mask, x_v, co_v, hr, part,
    m_v, a_v, b_v, s_v, k_v, snd, rcv, rts, rtr, hs,
    load_sem, small_sem, fs, fr, fl, bs, br, bl, hss, hrs,
):
    tile = lax.axis_index("tile")
    lev = lax.axis_index("lev")
    tiles = lax.axis_size("tile")

    barrier = pltpu.get_barrier_semaphore()
    for off in range(1, N):
        pl.semaphore_signal(barrier, inc=1, device_id=(tile, lax.rem(lev + off, N)), device_id_type=MESH)
    right, left = lax.rem(tile + 1, tiles), lax.rem(tile + tiles - 1, tiles)
    for t in (right, left):
        pl.semaphore_signal(barrier, inc=1, device_id=(t, lev), device_id_type=MESH)

    has_previous, has_next = tile != 0, tile != tiles - 1
    for way, has in ((0, has_previous), (1, has_next)):
        @pl.when(jnp.logical_not(has))
        def _():
            hr[way] = jnp.zeros((2, STACK, LANES), jnp.float32)

    def loads(i):
        rows = pl.ds(quarter_row(i), QUARTER)
        return (
            pltpu.make_async_copy(low.at[:, rows, :], a_v.at[:, rows, :], load_sem.at[i, 1]),
            pltpu.make_async_copy(upp.at[:, rows, :], b_v.at[:, rows, :], load_sem.at[i, 2]),
            pltpu.make_async_copy(adj.at[:, :, rows, :], m_v.at[:, :, rows, :], load_sem.at[i, 0]),
        )

    load_mask = pltpu.make_async_copy(mask, k_v, small_sem.at[0])
    load_sten = pltpu.make_async_copy(sten, s_v, small_sem.at[1])
    load_mask.start()
    for i in range(2):
        for c in loads(i):
            c.start()
    load_sten.start()

    @pl.when(lev == 0)
    def _():
        rtr[:, :, :FIELDS] = jnp.zeros((2, N, FIELDS, 8, LANES), jnp.float32)

    @pl.when(lev == N - 1)
    def _():
        rtr[:, :, FIELDS:] = jnp.zeros((2, N, FIELDS, 8, LANES), jnp.float32)

    first = jnp.where(lev == 0, 0.0, 1.0)
    last = jnp.where(lev == N - 1, 0.0, 1.0)

    def eliminate(i):
        for c in loads(i):
            c.wait()

        @pl.when(i < 2)
        def _():
            for c in loads(i + 2):
                c.start()

        start = quarter_row(i)
        rows = pl.ds(start, QUARTER)
        half, group = lax.div(i, 2), lax.rem(i, 2)
        keep = k_v[rows, :].astype(jnp.float32)
        r = [None] * FIELDS
        p = [None] * FIELDS
        a = a_v[0, rows, :] * first
        chain = a
        inv = g = q = b = None
        for k in range(LEVELS):
            b_next = b_v[k, rows, :]
            if k == LEVELS - 1:
                b_next = b_next * last
            d = 1.0 + a + b_next
            if k:
                d = d - b * a * inv
            inv = pltpu.reciprocal(d, approx=True)
            if k:
                h = b * inv
                g = h * g
                q = q + chain * g
            else:
                g = inv
                q = chain * g
            for f in range(FIELDS):
                m = m_v[f, k, rows, :] * keep
                if k:
                    r[f] = m * inv + h * r[f]
                    p[f] = p[f] + chain * r[f]
                else:
                    r[f] = m * inv
                    p[f] = chain * r[f]
                m_v[f, k, rows, :] = r[f]
            if k < LEVELS - 1:
                a = a_v[k + 1, rows, :]
                e = a * inv
            else:
                e = inv
            chain = chain * e
            a_v[k, rows, :] = e
            b_v[k, rows, :] = g
            b = b_next
        planes = [b * inv] + [b * r[f] for f in range(FIELDS)] + [chain, b * g, q] + p
        for j in range(4):
            row, col = (j // 2) * 8, (j % 2) * LANES
            for n, plane in enumerate(planes):
                snd[half, solver(group, j), n] = plane[row:row + 8, col:col + LANES]

    def forward(half, to, part):
        return pltpu.make_async_remote_copy(
            src_ref=snd.at[half, to, part], dst_ref=rcv.at[half, lev, part], send_sem=fs.at[half, to],
            recv_sem=fr.at[half, lev], device_id=(tile, to), device_id_type=MESH)

    def forward_from(half, source, part):
        return pltpu.make_async_remote_copy(
            src_ref=snd.at[half, source, part], dst_ref=rcv.at[half, source, part], send_sem=fs.at[half, source],
            recv_sem=fr.at[half, source], device_id=(tile, source), device_id_type=MESH)

    def backward(half, to, part):
        return pltpu.make_async_remote_copy(
            src_ref=rts.at[half, to, part], dst_ref=rtr.at[half, lev, part], send_sem=bs.at[half, to],
            recv_sem=br.at[half, lev], device_id=(tile, to), device_id_type=MESH)

    def backward_from(half, source, part):
        return pltpu.make_async_remote_copy(
            src_ref=rts.at[half, source, part], dst_ref=rtr.at[half, source, part], send_sem=bs.at[half, source],
            recv_sem=br.at[half, source], device_id=(tile, source), device_id_type=MESH)

    def own_forward(half):
        return pltpu.make_async_copy(snd.at[half, lev], rcv.at[half, lev], fl.at[half])

    def own_backward(half):
        return pltpu.make_async_copy(rts.at[half, lev], rtr.at[half, lev], bl.at[half])

    def by_slab(s, parts, run):
        pl.when(s == 0)(lambda: run(parts[0]))
        pl.when(s == N - 1)(lambda: run(parts[2]))
        pl.when((s != 0) & (s != N - 1))(lambda: run(parts[1]))

    def send_forward(i):
        half, group = lax.div(i, 2), lax.rem(i, 2)

        def run(part):
            for dx, dz in ((2, 1), (1, 1), (3, 1), (0, 1), (2, 0), (1, 0), (3, 0)):
                to = 2 * lax.rem(lax.div(lev, 2) + dx, 4) + lax.rem(lev + dz, 2)
                forward(half, to, part).start()

        by_slab(lev, FORWARD, run)
        own_forward(half).start()

    def quarter(i, carry):
        eliminate(i)
        pl.when(i == 1)(lambda: pl.semaphore_wait(barrier, N + 1))
        pl.when(lax.rem(i, 2) == 1)(lambda: send_forward(i))
        return carry

    load_mask.wait()
    lax.fori_loop(0, 4, quarter, 0)
    load_sten.wait()

    row = lax.broadcasted_iota(jnp.int32, (ROWS, LANES), 0)
    lane = lax.broadcasted_iota(jnp.int32, (ROWS, LANES), 1)
    has_left = jnp.where(tile == 0, 0.0, 1.0)
    has_right = jnp.where(tile == tiles - 1, 0.0, 1.0)
    for c in range(2):
        cols = pl.ds(c * LANES, LANES)
        east, west, north, south = s_v[0, :, cols], s_v[1, :, cols], s_v[2, :, cols], s_v[3, :, cols]
        co_v[0, c] = 1.0 - (east + west + north + south)
        co_v[1, c] = jnp.where(row == 0, has_left, pltpu.roll(east, 1, 0))
        co_v[2, c] = jnp.where(row == ROWS - 1, has_right, pltpu.roll(west, ROWS - 1, 0))
        before = 0.0 if c == 0 else pltpu.roll(s_v[2, :, :LANES], 1, 1)
        after = pltpu.roll(s_v[3, :, LANES:], LANES - 1, 1) if c == 0 else 0.0
        co_v[3, c] = jnp.where(lane == 0, before, pltpu.roll(north, 1, 1))
        co_v[4, c] = jnp.where(lane == LANES - 1, after, pltpu.roll(south, LANES - 1, 1))

    def clear(n, carry):
        for r in (-PAD, QUARTER, ROWS - QUARTER - 8, ROWS):
            x_v[pl.ds(pl.multiple_of(n * HEIGHT + PAD + r, 8), 8), :] = jnp.zeros((8, LANES), jnp.float32)
        return carry

    lax.fori_loop(0, 2 * STACK, clear, 0, unroll=8)

    def solve(half, carry):
        own_forward(half).wait()
        for s in range(N):
            part = FORWARD[0 if s == 0 else 2 if s == N - 1 else 1]
            pl.when(lev != s)(lambda: forward_from(half, s, part).wait_recv())
        fields = range(FIELDS)
        flux = [rcv[half, 0, 1 + f] for f in fields]
        slope = rcv[half, 0, 0]
        into, gain = [None] * N, [None] * N
        for s in range(1, N):
            aa = rcv[half, s, 7]
            inv = pltpu.reciprocal(1.0 - slope * aa, approx=True)
            into[s] = [(flux[f] + slope * rcv[half, s, 8 + f]) * inv for f in fields]
            if s < N - 1:
                dd, bb, cc = rcv[half, s, 0], rcv[half, s, 5], rcv[half, s, 6]
                gain[s] = slope * bb * inv
                flux = [rcv[half, s, 1 + f] + cc * into[s][f] for f in fields]
                slope = dd + cc * gain[s]
        zero = jnp.zeros((8, LANES), jnp.float32)
        v = [zero] * FIELDS
        for s in range(N - 1, -1, -1):
            if s == 0:
                u = [zero] * FIELDS
            elif s == N - 1:
                u = into[s]
            else:
                u = [into[s][f] + gain[s] * v[f] for f in fields]
            for f in fields:
                rts[half, s, f] = u[f]
                rts[half, s, FIELDS + f] = v[f]
            if s:
                w = [rcv[half, s, 8 + f] + rcv[half, s, 7] * u[f] for f in fields]
                v = w if s == N - 1 else [w[f] + rcv[half, s, 5] * v[f] for f in fields]
        own_backward(half).start()
        for dx, dz in ((2, 1), (1, 1), (3, 1), (0, 1), (2, 0), (1, 0), (3, 0)):
            to = 2 * lax.rem(lax.div(lev, 2) + dx, 4) + lax.rem(lev + dz, 2)
            by_slab(to, BACKWARD, lambda part: backward(half, to, part).start())
        return carry

    lax.fori_loop(0, 2, solve, 0)

    def returned(half, sources):
        def run(part):
            for s in sources:
                pl.when(lev != s)(lambda: backward_from(half, s, part).wait_recv())

        by_slab(lev, BACKWARD, run)
        for s in sources:
            pl.when(lev == s)(lambda: own_backward(half).wait())

    def substitute(half, j, way=None):
        start = pl.multiple_of(quarter_row(half * 2 + lax.div(j, 2)) + 8 * lax.rem(j, 2), 8)
        rows = pl.ds(start, 8)
        if way is not None:
            edge = 0 if way else ROWS - 1
            weight = [s_v[way, edge:edge + 1, c * LANES:(c + 1) * LANES] for c in range(2)]
        for c in range(2):
            cols = pl.ds(c * LANES, LANES)
            source = solver(lax.div(j, 2), 2 * lax.rem(j, 2) + c)
            x = [None] * FIELDS
            for k in range(LEVELS - 1, -1, -1):
                e, g = a_v[k, rows, cols], b_v[k, rows, cols]
                for f in range(FIELDS):
                    u = rtr[half, source, f]
                    beyond = rtr[half, source, FIELDS + f] if k == LEVELS - 1 else x[f]
                    x[f] = m_v[f, k, rows, cols] + g * u + e * beyond
                    x_v[pl.ds(pl.multiple_of(spot(f * LEVELS + k, c, start), 8), 8), :] = x[f]
                    if way is not None:
                        edge = 0 if way else 7
                        hs[way, c, pl.ds(f * LEVELS + k, 1), :] = x[f][edge:edge + 1, :] * weight[c]

    def halo(way):
        to = right if way == 0 else left
        return pltpu.make_async_remote_copy(
            src_ref=hs.at[way], dst_ref=hr.at[way], send_sem=hss.at[way], recv_sem=hrs.at[way],
            device_id=(to, lev), device_id_type=MESH)

    def blocks(half, first, count, step):
        def body(n, carry):
            substitute(half, first + n * step)
            return carry

        lax.fori_loop(0, count, body, 0, unroll=2)

    for way, j, tiles_of in ((1, 0, (0, 1)), (0, 3, (2, 3))):
        returned(0, [solver_of(j // 2, n) for n in tiles_of])
        substitute(0, j, way)
        has = has_next if way == 0 else has_previous
        pl.when(has)(lambda: halo(way).start())
    returned(0, [solver_of(0, 2), solver_of(0, 3), solver_of(1, 0), solver_of(1, 1)])
    blocks(0, 1, 2, 1)
    lax.fori_loop(0, 2, lambda j, carry: transport(x_v, co_v, part, j * (ROWS - QUARTER), j * QUARTER), 0)
    returned(1, range(N))
    blocks(1, 0, 4, 1)
    transport(x_v, co_v, part, QUARTER, 2 * QUARTER)
    for way in range(2):
        to, of = (has_next, has_previous) if way == 0 else (has_previous, has_next)
        pl.when(of)(lambda: halo(way).wait_recv())
        pl.when(to)(lambda: halo(way).wait_send())

    def drain(part):
        for half in range(2):
            for off in range(1, N):
                forward(half, lax.rem(lev + off, N), part).wait_send()

    by_slab(lev, FORWARD, drain)
    for half in range(2):
        for off in range(1, N):
            to = lax.rem(lev + off, N)
            by_slab(to, BACKWARD, lambda part: backward(half, to, part).wait_send())


def per_device(adjoint_state, lower_coef, upper_coef, stencil_coef, land_mask):
    f32 = jnp.float32
    dma = pltpu.SemaphoreType.DMA
    space = pltpu.VMEM
    fields, slab, rows, cols = adjoint_state.shape
    parts = pl.pallas_call(
        kernel,
        out_shape=[
            space((STACK * 2 * HEIGHT, LANES), f32),
            space((5, 2, ROWS, LANES), f32),
            space((2, 2, STACK, LANES), f32),
            space((fields, slab, 3 * QUARTER, cols), f32),
        ],
        in_specs=[pl.BlockSpec(memory_space=pltpu.HBM)] * 5,
        out_specs=[pl.BlockSpec(memory_space=space)] * 4,
        scratch_shapes=[
            space((FIELDS, LEVELS, ROWS, COLS), f32),
            space((LEVELS, ROWS, COLS), f32),
            space((LEVELS, ROWS, COLS), f32),
            space((4, ROWS, COLS), f32),
            space((ROWS, COLS), jnp.int32),
            space((2, N, PLANES, 8, LANES), f32),
            space((2, N, PLANES, 8, LANES), f32),
            space((2, N, BACK, 8, LANES), f32),
            space((2, N, BACK, 8, LANES), f32),
            space((2, 2, STACK, LANES), f32),
            dma((4, 3)),
            dma((2,)),
            dma((2, N)),
            dma((2, N)),
            dma((2,)),
            dma((2, N)),
            dma((2, N)),
            dma((2,)),
            dma((2,)),
            dma((2,)),
        ],
        compiler_params=pltpu.CompilerParams(
            collective_id=0, has_side_effects=True, vmem_limit_bytes=32 * 2**20),
    )(*(pltpu.with_memory_space_constraint(x, pltpu.HBM) for x in (
        adjoint_state, lower_coef, upper_coef, stencil_coef, land_mask)))
    return pl.pallas_call(
        finish,
        out_shape=jax.ShapeDtypeStruct(adjoint_state.shape, f32),
        in_specs=[pl.BlockSpec(memory_space=space)] * 4,
        out_specs=pl.BlockSpec(memory_space=pltpu.HBM),
        scratch_shapes=[space(adjoint_state.shape, f32), dma((4,))],
        compiler_params=pltpu.CompilerParams(vmem_limit_bytes=16 * 2**20),
    )(*(pltpu.with_memory_space_constraint(x, space) for x in parts))


def solution(mesh):
    return jax.shard_map(
        per_device,
        mesh=mesh,
        in_specs=(
            P(None, "lev", "tile", None),
            P("lev", "tile", None),
            P("lev", "tile", None),
            P(None, "tile", None),
            P("tile", None),
        ),
        out_specs=P(None, "lev", "tile", None),
        check_vma=False,
    )
```
